256 devices in a mesh: store: 4 (over y_hi, core), req: 8 (over z), tp: 8 (over y_lo, x).
Axes of the slice: x: 4, y: 4 (y_hi: 2, y_lo: 2; y = y_hi * 2 + y_lo), z: 8, core: 2. Of those that a mesh axis runs over, the one named last changes fastest.
Arguments:
- hidden: bfloat16 [4096, 9216], P('store', 'req'), may hold values from -6 to 6
- row_counts: int32 [4], replicated, may hold values from 128 to 1024, as said below
- ln_gain: float32 [9216], P('req'), may hold values from 0.1 to 1.9
- ln_bias: float32 [9216], P('req'), may hold values from -3 to 3
- key_weight: bfloat16 [9216, 5120], P('req', 'tp'), may hold values from -0.0625 to 0.0625
- value_weight: bfloat16 [9216, 5120], P('req', 'tp'), may hold values from -0.0625 to 0.0625
- suffix_q: bfloat16 [128, 128, 5120], P(('store', 'req'), None, 'tp'), may hold values from -192 to 192
- suffix_k: bfloat16 [128, 128, 5120], P(('store', 'req'), None, 'tp'), may hold values from -4.6 to 4.6
- suffix_v: bfloat16 [128, 128, 5120], P(('store', 'req'), None, 'tp'), may hold values from -6 to 6
- suffix_lengths: int32 [128], P(('store', 'req')), may hold values from 1 to 128, 8192 in all
Outputs:
- context: bfloat16 [128, 128, 5120], P(('store', 'req'), None, 'tp')
The draws below stay inside these ranges and needn't reach their ends.
Inputs may be any that keep to these rules, and one draw needn't show every extreme that they name: Owner o holds transcript rows in its first row_counts[o] slots; each count is a multiple of 128, the counts sum to 2048, and one owner is full with 1024. Request r's suffix fills its first suffix_lengths[r] slots; the lengths sum to 8192.
All inputs are finite; a program needn't handle non-finite values. No bound on the sum of `suffix_lengths` on one device may be relied on, other than what follows from the above.
Results may differ from the reference program's by a relative error of at most 0.0039.
Values may be sent and summed in bfloat16 or wider, within the bound.
No kernel may reach another device: no remote copies, remote signals or barrier semaphores. Data moves between devices by JAX's collectives and lax.ppermute only.
A program may use at most 128 MiB of HBM per device.

```python
import math
import jax
import jax.numpy as jnp
import numpy as np
from jax import lax

D = 9216
HD = 128
HEADS = 40
CAP = 1024
SUF = 128
REQS = 128
N_STORE = 4


def shared_pair(key, boost):
    key_query, key_keys = jax.random.split(key)
    base_query = jnp.clip(jax.random.normal(key_query, (REQS, SUF, HEADS * HD), jnp.float32), -4.5, 4.5)
    base_keys = jnp.clip(jax.random.normal(key_keys, (REQS, SUF, HEADS * HD), jnp.float32), -4.5, 4.5)
    position = jnp.arange(SUF, dtype=jnp.int32)
    chosen = (position % 16 == 15).astype(jnp.float32) * boost
    strength = 10.0 * jnp.power(2.0, (position // 16 % 3).astype(jnp.float32))
    spacing = 2.0 / (strength * math.sqrt(HD))
    queries = base_query * (1.0 - chosen)[None, :, None]
    chosen_next = jnp.roll(chosen, -1)
    spacing_next = jnp.roll(spacing, -1)
    keys_next = jnp.roll(base_keys, -1, axis=1)
    new_keys = base_keys * (1.0 - chosen_next)[None, :, None] + (chosen_next * (1.0 + spacing_next))[None, :, None] * keys_next
    return (queries, new_keys)


def draw_suffix_q(key, part):
    return shared_pair(key, 0.0)[0].astype(jnp.bfloat16)


def draw_suffix_k(key, part):
    return shared_pair(key, 0.0)[1].astype(jnp.bfloat16)


def draw_row_counts(key, part):
    key = jax.random.fold_in(key, 5)
    key_first, key_second, key_order = jax.random.split(key, 3)
    blocks_full = CAP // 128
    first_share = jax.random.randint(key_first, (), 1, blocks_full - 1)
    second_share = jax.random.randint(key_second, (), 1, blocks_full - first_share)
    third_share = blocks_full - first_share - second_share
    shares = jnp.stack([jnp.int32(blocks_full), first_share.astype(jnp.int32), second_share.astype(jnp.int32), third_share.astype(jnp.int32)])
    order = jax.random.permutation(key_order, 4)
    return (shares[order] * 128).astype(jnp.int32)


def level_of(stream_key, dims, pieces, smallest, largest):
    loudness = 1.0
    for axis_at, parts in pieces:
        draws = jax.random.uniform(jax.random.fold_in(jax.random.fold_in(stream_key, 6), axis_at), (parts,), jnp.float32, smallest / len(pieces), largest / len(pieces))
        loudness = loudness * jnp.repeat(jnp.exp(draws), dims[axis_at] // parts).reshape((-1,) + (1,) * (len(dims) - 1 - axis_at))
    return loudness


def profile(amount, total, reach, skew):
    portions = [(1 << 20) // math.isqrt(standing ** skew) + 1 for standing in range(2, amount + 1)]
    rest, given = total - reach - (amount - 1), [1] * (amount - 1)
    while rest > 0:
        candidates = [i for i in range(amount - 1) if given[i] < reach]
        pool, remaining = sum([portions[i] for i in candidates]), rest
        for i in candidates:
            extra = min(reach - given[i], max(1, remaining * portions[i] // pool), rest)
            given[i] = given[i] + extra
            rest = rest - extra
    return np.array([reach] + given)


def uneven(stream_key, amount, total, reach, slope):
    if amount == 2:
        one = jax.random.randint(stream_key, (), max(1, total - reach), min(reach, total - 1) + 1)
        return jnp.stack([one, total - one])
    sizes = jnp.asarray(profile(amount, total, reach, slope), jnp.int32)
    couples = (amount - 1) // 2
    donor, receiver = sizes[1:1 + 2 * couples:2], sizes[2:2 + 2 * couples:2]
    room = jnp.minimum(donor - 1, reach - receiver)
    passed = jax.random.randint(jax.random.fold_in(stream_key, 1), (couples,), 0, 1 << 20) % (room + 1)
    sizes = sizes.at[1:1 + 2 * couples:2].set(donor - passed).at[2:2 + 2 * couples:2].set(receiver + passed)
    return sizes[jax.random.permutation(jax.random.fold_in(stream_key, 2), amount)]


def bell_draw(rng, dims, deviation, bound, shards=(), kind=jnp.bfloat16):
    array = jax.random.normal(rng, dims, jnp.float32) * deviation
    if len(shards) > 0:
        array = level_of(rng, dims, shards, -0.22, 0.18) * array
    return jnp.clip(array, min=-bound, max=bound).astype(kind)


def setup_inputs(seed: int = 0) -> dict:
    arg_keys = jax.random.split(jax.random.key(seed), 11)
    hidden = bell_draw(arg_keys[0], (N_STORE * CAP, D), 1.0, 6.0, ((0, 4), (1, 8)))
    row_counts = draw_row_counts(jax.random.fold_in(arg_keys[10], 71), 0)
    ln_gain = jnp.clip(1.0 + 0.18 * jax.random.normal(arg_keys[2], (D,), jnp.float32), 0.1, 1.9)
    ln_bias = bell_draw(arg_keys[3], (D,), 0.5, 3.0, ((0, 8),), jnp.float32)
    key_weight = bell_draw(arg_keys[4], (D, HEADS * HD), D ** -0.5, 0.0625, ((0, 8), (1, 8)))
    value_weight = bell_draw(arg_keys[5], (D, HEADS * HD), D ** -0.5, 0.0625, ((0, 8), (1, 8)))
    suffix_q = draw_suffix_q(jax.random.fold_in(arg_keys[10], 71), 0)
    suffix_k = draw_suffix_k(jax.random.fold_in(arg_keys[10], 71), 0)
    suffix_v = bell_draw(arg_keys[8], (REQS, SUF, HEADS * HD), 1.0, 6.0, ((0, 32), (2, 8)))
    suffix_lengths = uneven(arg_keys[9], REQS, REQS * SUF // 2, SUF, 2).astype(jnp.int32)
    return dict(hidden=hidden, row_counts=row_counts, ln_gain=ln_gain, ln_bias=ln_bias, key_weight=key_weight, value_weight=value_weight, suffix_q=suffix_q, suffix_k=suffix_k, suffix_v=suffix_v, suffix_lengths=suffix_lengths)


epsilon = 1e-05

def reference(hidden, row_counts, ln_gain, ln_bias, key_weight, value_weight, suffix_q, suffix_k, suffix_v, suffix_lengths):
    row_ids = jnp.arange(N_STORE * CAP, dtype=jnp.int32)
    holder = row_ids // CAP
    live_rows = row_ids - holder * CAP < row_counts[holder]
    widened = hidden.astype(jnp.float32)
    row_mean = lax.optimization_barrier(jnp.sum(widened, axis=1)) / D
    row_var = lax.optimization_barrier(jnp.sum(widened * widened, axis=1)) / D - row_mean * row_mean
    normed = ((widened - row_mean[:, None]) * lax.rsqrt(row_var + epsilon)[:, None] * ln_gain + ln_bias).astype(jnp.bfloat16)
    prefix_keys = jnp.dot(normed, key_weight, preferred_element_type=jnp.float32).astype(jnp.bfloat16)
    prefix_values = jnp.dot(normed, value_weight, preferred_element_type=jnp.float32).astype(jnp.bfloat16)
    key_heads = prefix_keys.astype(jnp.float32).reshape(N_STORE * CAP, HEADS, HD)
    value_heads = prefix_values.astype(jnp.float32).reshape(N_STORE * CAP, HEADS, HD)
    score_scale = 1.0 / math.sqrt(HD)
    causal = jnp.arange(SUF)[None, :] <= jnp.arange(SUF)[:, None]

    def one_request(entry):
        query_in, key_in, value_in, length = entry
        queries = query_in.astype(jnp.float32).reshape(SUF, HEADS, HD)
        own_keys = key_in.astype(jnp.float32).reshape(SUF, HEADS, HD)
        own_values = value_in.astype(jnp.float32).reshape(SUF, HEADS, HD)
        prefix_scores = jnp.einsum('qhd,khd->qhk', queries, key_heads) * score_scale
        prefix_scores = jnp.where(live_rows[None, None, :], prefix_scores, -jnp.inf)
        own_scores = jnp.einsum('qhd,khd->qhk', queries, own_keys) * score_scale
        own_scores = jnp.where(causal[:, None, :], own_scores, -jnp.inf)
        top = jnp.maximum(lax.optimization_barrier(jnp.max(prefix_scores, axis=-1)), lax.optimization_barrier(jnp.max(own_scores, axis=-1)))
        prefix_weights = lax.optimization_barrier(jnp.exp(prefix_scores - top[..., None]).astype(jnp.bfloat16)).astype(jnp.float32)
        own_weights = lax.optimization_barrier(jnp.exp(own_scores - top[..., None]).astype(jnp.bfloat16)).astype(jnp.float32)
        total = lax.optimization_barrier(jnp.sum(prefix_weights, axis=-1)) + lax.optimization_barrier(jnp.sum(own_weights, axis=-1))
        mixed = jnp.einsum('qhk,khd->qhd', prefix_weights, value_heads) + jnp.einsum('qhk,khd->qhd', own_weights, own_values)
        mixed = mixed / total[..., None]
        live_queries = jnp.arange(SUF, dtype=jnp.int32) < length
        mixed = jnp.where(live_queries[:, None, None], mixed, 0.0)
        return mixed.astype(jnp.bfloat16).reshape(SUF, HEADS * HD)
    return lax.map(one_request, (suffix_q, suffix_k, suffix_v, suffix_lengths))
```

```python
import functools
import math

import jax
import jax.numpy as jnp
from jax import lax
from jax.experimental import pallas as pl
from jax.experimental.pallas import tpu as pltpu
from jax.sharding import PartitionSpec as P

HD = 128
UNIT = 128
epsilon = 1e-05
MIB = 1 << 20


def projection_kernel(
    span, scalars, hidden, extra, gain, bias, key_weight, value_weight, *rest
):
    outs, (sums, sums_extra, moments, moments_extra) = rest[:8], rest[8:]
    own, half, extra_at, extra_rows, me = (scalars[i] for i in range(5))
    width = hidden.shape[1]
    cols = key_weight.shape[1]
    weights = ((key_weight, 0), (value_weight, cols))

    row_id = lax.broadcasted_iota(jnp.int32, (16, width), 0)
    affine = jnp.where(row_id == 2, gain[...], jnp.where(row_id == 3, bias[...], 0.0))
    first = affine.astype(jnp.bfloat16)
    left = affine - first.astype(jnp.float32)
    second = left.astype(jnp.bfloat16)
    third = (left - second.astype(jnp.float32)).astype(jnp.bfloat16)
    affine_sums = []
    for weight, _ in weights:
        affine_sums.append(
            sum(
                jnp.dot(piece, weight[...], preferred_element_type=jnp.float32)
                for piece in (first, second, third)
            )
        )

    def project(rows, total, moment, start, count):
        wide = rows.astype(jnp.float32)
        row_sum = jnp.sum(wide, axis=1, keepdims=True)
        row_square = jnp.sum(wide * wide, axis=1, keepdims=True)
        centre = row_sum * (1.0 / width)
        scaled = ((wide - centre) * gain[...]).astype(jnp.bfloat16)
        for (weight, at), affine_sum in zip(weights, affine_sums):
            total[pl.ds(start, count), at : at + cols] = (
                jnp.dot(scaled, weight[...], preferred_element_type=jnp.float32)
                + centre * affine_sum[2:3]
            )
        lane = lax.broadcasted_iota(jnp.int32, (count, 128), 1)
        moment[pl.ds(start, count), :] = jnp.where(
            lane == 0, row_sum, jnp.where(lane == 1, row_square, 0.0)
        )

    tile = 256

    def one_tile(t, carry):
        start = pl.multiple_of(t * tile, tile)
        project(hidden[pl.ds(start, tile), :], sums, moments, start, tile)
        return carry

    lax.fori_loop(0, (jnp.minimum(own, half) + tile - 1) // tile, one_tile, 0)

    @pl.when(extra_rows > 0)
    def _():
        count = extra.shape[0] // 2
        for t in range(2):
            project(
                extra[t * count : (t + 1) * count, :], sums_extra, moments_extra, t * count, count
            )

        def one_move(u, carry):
            source = pl.multiple_of(extra_at + u * 64, 64)
            target = pl.multiple_of(own + u * 64, 64)
            sums[pl.ds(target, 64), :] = sums_extra[pl.ds(source, 64), :]
            moments[pl.ds(target, 64), :] = moments_extra[pl.ds(source, 64), :]
            return carry

        lax.fori_loop(0, extra_rows // 64, one_move, 0)

    share = half // 8
    small_id = lax.broadcasted_iota(jnp.int32, (8, cols), 0)
    for d, out in enumerate(outs):
        target = lax.rem(me + d, 8)
        start = pl.multiple_of(target * share, 8)
        out[0:span, :] = sums[pl.ds(start, span), :]
        flipped = jnp.transpose(moments[pl.ds(start, 128), :])[0:8]
        for (_, at), affine_sum in zip(weights, affine_sums):
            tail = jnp.where(
                jnp.logical_or(small_id == 2, small_id == 3), affine_sum[0:8], 0.0
            )
            out[span : span + 8, at : at + cols] = tail
            if at == 0:
                out[span : span + 8, 0:128] = jnp.where(
                    small_id[:, 0:128] < 2, flipped, tail[:, 0:128]
                )


def project_rows(span, scalars, hidden, extra, gain, bias, key_weight, value_weight):
    capacity, width = hidden.shape
    cols = key_weight.shape[1]
    vmem = pl.BlockSpec(memory_space=pltpu.VMEM)
    return pl.pallas_call(
        functools.partial(projection_kernel, span),
        out_shape=[jax.ShapeDtypeStruct((span + 8, 2 * cols), jnp.float32)] * 8,
        in_specs=[pl.BlockSpec(memory_space=pltpu.SMEM)] + [vmem] * 6,
        out_specs=[vmem] * 8,
        scratch_shapes=[
            pltpu.VMEM((capacity, 2 * cols), jnp.float32),
            pltpu.VMEM((extra.shape[0], 2 * cols), jnp.float32),
            pltpu.VMEM((capacity, 128), jnp.float32),
            pltpu.VMEM((extra.shape[0], 128), jnp.float32),
        ],
        compiler_params=pltpu.CompilerParams(vmem_limit_bytes=44 * MIB),
        cost_estimate=pl.CostEstimate(
            flops=2 * capacity * width * 2 * cols, bytes_accessed=12 * MIB, transcendentals=0
        ),
    )(scalars, hidden, extra, gain, bias, key_weight, value_weight)


def attention_kernel(key_count, lengths, q, own_k, own_v, *rest):
    keys, values, out = rest[:key_count], rest[key_count:-1], rest[-1]
    requests, positions, _ = q.shape
    rows = requests * positions
    rate = math.log2(math.e) / math.sqrt(HD)
    ones = jnp.ones((512, HD), jnp.bfloat16)

    def scores_of(queries, block):
        return lax.dot_general(
            queries, block, (((1,), (1,)), ((), ())), preferred_element_type=jnp.float32
        )

    def weigh(scores, top, block):
        weights = jnp.exp2((scores - top) * rate).astype(jnp.bfloat16)
        both = jnp.concatenate([block, ones[: block.shape[0]]], axis=1)
        return jnp.dot(weights, both, preferred_element_type=jnp.float32)

    row = lax.broadcasted_iota(jnp.int32, (positions, positions), 0)
    column = lax.broadcasted_iota(jnp.int32, (positions, positions), 1)
    tops, sums = [], []
    for r in range(requests):
        scores = jnp.where(column <= row, scores_of(q[r], own_k[r]), -jnp.inf)
        top = jnp.max(scores, axis=1, keepdims=True)
        tops.append(top)
        sums.append(weigh(scores, top, own_v[r]))
    top = jnp.concatenate(tops, axis=0)
    total = jnp.concatenate(sums, axis=0)
    queries = q[...].reshape(rows, HD)
    for at in range(0, key_count, 4):
        block = jnp.concatenate([keys[i][...] for i in range(at, at + 4)], axis=0)
        scores = scores_of(queries, block)
        top_next = jnp.maximum(top, jnp.max(scores, axis=1, keepdims=True))
        factor = jnp.exp2((top - top_next) * rate)
        block = jnp.concatenate([values[i][...] for i in range(at, at + 4)], axis=0)
        total = total * factor + weigh(scores, top_next, block)
        top = top_next
    result = total[:, :HD] / total[:, HD:]
    place = lax.broadcasted_iota(jnp.int32, (positions, HD), 0)
    for r in range(requests):
        live = place < lengths[r]
        part = result[r * positions : (r + 1) * positions]
        out[r] = jnp.where(live, part, 0.0).astype(jnp.bfloat16)


def attend(lengths, q, own_k, own_v, keys, values):
    requests, positions, width = q.shape
    heads = width // HD
    whole = pl.BlockSpec((requests, positions, HD), lambda h: (0, 0, h))

    def piece(item):
        array, at = item
        return pl.BlockSpec((array.shape[0], HD), lambda h, at=at: (0, at + h))

    return pl.pallas_call(
        functools.partial(attention_kernel, len(keys)),
        grid=(heads,),
        out_shape=jax.ShapeDtypeStruct(q.shape, jnp.bfloat16),
        in_specs=[pl.BlockSpec(memory_space=pltpu.SMEM)]
        + [whole] * 3
        + [piece(item) for item in keys + values],
        out_specs=whole,
        compiler_params=pltpu.CompilerParams(vmem_limit_bytes=44 * MIB),
        cost_estimate=pl.CostEstimate(
            flops=4 * requests * positions * 2048 * width,
            bytes_accessed=8 * MIB,
            transcendentals=requests * positions * 2048 * heads,
        ),
    )(lengths, q, own_k, own_v, *[array for array, _ in keys + values])


def per_device(
    hidden,
    row_counts,
    ln_gain,
    ln_bias,
    key_weight,
    value_weight,
    suffix_q,
    suffix_k,
    suffix_v,
    suffix_lengths,
):
    capacity = hidden.shape[0]
    cols = key_weight.shape[1]
    heads = cols // HD
    store = lax.axis_index("store")
    me = lax.axis_index("req")
    ring = lax.axis_size("req")
    depth = ring * key_weight.shape[0]
    up = [(i, (i + 1) % ring) for i in range(ring)]
    down = [(i, (i - 1) % ring) for i in range(ring)]
    cores = [(0, 1), (1, 0), (2, 3), (3, 2)]
    far = [(0, 2), (1, 3), (2, 0), (3, 1)]

    pair = lax.dynamic_slice(row_counts, (store // 2 * 2,), (2,))
    own = lax.dynamic_index_in_dim(row_counts, store, keepdims=False)
    chip_rows = pair[0] + pair[1]
    half = chip_rows // 2
    spare = 7 * UNIT // 2
    first_sent = jnp.minimum(half, capacity - spare)
    extra = lax.ppermute(
        lax.dynamic_slice(hidden, (first_sent, 0), (spare, hidden.shape[1])), "store", cores
    )
    scalars = jnp.stack(
        [own, half, half - first_sent, jnp.maximum(half - own, 0), me]
    ).astype(jnp.int32)

    def reduced(span):
        def run(scalars, hidden, extra, gain, bias, key_weight, value_weight):
            parts = project_rows(
                span, scalars, hidden, extra, gain, bias, key_weight, value_weight
            )
            going_up = lax.ppermute(parts[4][:, :cols], "req", up)
            going_down = lax.ppermute(parts[4][:, cols:], "req", down)
            going_up = jnp.concatenate(
                [parts[3][:, :cols] + going_up, parts[3][:, cols:]], axis=1
            )
            going_down = jnp.concatenate(
                [parts[5][:, :cols], parts[5][:, cols:] + going_down], axis=1
            )
            going_up = lax.ppermute(going_up, "req", up) + parts[2]
            going_down = lax.ppermute(going_down, "req", down) + parts[6]
            going_up = lax.ppermute(going_up, "req", up) + parts[1]
            going_down = lax.ppermute(going_down, "req", down) + parts[7]
            total = (
                lax.ppermute(going_up, "req", up)
                + lax.ppermute(going_down, "req", down)
                + parts[0]
            )
            mean = total[span, :span] / depth
            var = total[span + 1, :span] / depth - mean * mean
            rows = (total[:span] - mean[:, None] * total[span + 2][None, :]) * lax.rsqrt(
                var + epsilon
            )[:, None] + total[span + 3][None, :]
            rows = rows.astype(jnp.bfloat16)
            return jnp.pad(rows, ((0, 112 - span), (0, 0)))

        return run

    most = jnp.maximum(row_counts[0] + row_counts[1], row_counts[2] + row_counts[3]) // UNIT
    rows = lax.switch(
        jnp.clip(most - 9, 0, 5),
        [reduced(8 * units) for units in range(9, 15)],
        scalars,
        hidden,
        extra,
        ln_gain[None, :],
        ln_bias[None, :],
        key_weight,
        value_weight,
    )
    rows_far = lax.ppermute(rows, "store", far)
    block = jnp.pad(rows, ((0, 240 - 112), (0, 0)))
    block = lax.dynamic_update_slice(block, rows_far, (chip_rows // 16, 0))[:128]

    full = [block]
    going_up = going_down = block
    for _ in range(3):
        going_up = lax.ppermute(going_up, "req", up)
        going_down = lax.ppermute(going_down, "req", down)
        full += [going_up, going_down]
    last_k = lax.ppermute(going_up[:, :cols], "req", up)
    last_v = lax.ppermute(going_down[:, cols:], "req", down)
    full += [lax.ppermute(piece, "store", cores) for piece in full]
    keys = [(piece, 0) for piece in full]
    values = [(piece, heads) for piece in full]
    keys += [(last_k, 0), (lax.ppermute(last_k, "store", cores), 0)]
    values += [(last_v, 0), (lax.ppermute(last_v, "store", cores), 0)]
    return attend(suffix_lengths, suffix_q, suffix_k, suffix_v, keys, values)


def solution(mesh):
    in_specs = (
        P("store", "req"),
        P(),
        P("req"),
        P("req"),
        P("req", "tp"),
        P("req", "tp"),
        P(("store", "req"), None, "tp"),
        P(("store", "req"), None, "tp"),
        P(("store", "req"), None, "tp"),
        P(("store", "req")),
    )
    out_specs = P(("store", "req"), None, "tp")
    return jax.shard_map(
        per_device, mesh=mesh, in_specs=in_specs, out_specs=out_specs, check_vma=False
    )
```

```python
import functools
import math

import jax
import jax.numpy as jnp
from jax import lax
from jax.experimental import pallas as pl
from jax.experimental.pallas import tpu as pltpu
from jax.sharding import PartitionSpec as P

HD = 128
UNIT = 128
MOST_UNITS = 14
SPAN = 16 * MOST_UNITS
TAIL = 8
epsilon = 1e-05
MIB = 1 << 20


def projection_kernel(
    counts, hidden, hidden_other, gain, bias, key_weight, value_weight, *rest
):
    parts, (rows_in, semaphores) = rest[:5], rest[5:]
    store = lax.axis_index("store")
    me = lax.axis_index("req")
    core = lax.rem(store, 2)
    first_count = counts[store - core]
    second_count = counts[store - core + 1]
    share = (first_count + second_count) // 8
    width = hidden.shape[1]
    cols = key_weight.shape[1]
    weights = (key_weight, value_weight)

    def copies(act):
        for side, source in enumerate((hidden, hidden_other)):
            first = (core + side) % 2 == 0
            count = jnp.where(first, first_count, second_count)
            base = jnp.where(first, 0, first_count)
            for unit in range(source.shape[0] // UNIT):

                @pl.when(unit * UNIT < count)
                def _():
                    at = pl.multiple_of(base + unit * UNIT, UNIT)
                    act(
                        pltpu.make_async_copy(
                            source.at[pl.ds(unit * UNIT, UNIT)],
                            rows_in.at[pl.ds(at, UNIT)],
                            semaphores.at[side, unit],
                        )
                    )

    copies(lambda copy: copy.start())

    row_id = lax.broadcasted_iota(jnp.int32, (16, width), 0)
    affine = jnp.where(row_id == 2, gain[...], jnp.where(row_id == 3, bias[...], 0.0))
    pieces = []
    left = affine
    for _ in range(3):
        piece = left.astype(jnp.bfloat16)
        pieces.append(piece)
        left = left - piece.astype(jnp.float32)
    affine_sums = [
        sum(
            jnp.dot(piece, weight[...], preferred_element_type=jnp.float32) for piece in pieces
        )
        for weight in weights
    ]
    copies(lambda copy: copy.wait())

    tail_row = lax.broadcasted_iota(jnp.int32, (TAIL, cols), 0)
    lane = lax.broadcasted_iota(jnp.int32, (128, 128), 1)

    def project(part, steps, halves):
        target = lax.rem(me + jnp.where(core == 0, steps, 8 - steps), 8)
        start = pl.multiple_of(target * share, 16)
        wide = rows_in[pl.ds(start, SPAN), :].astype(jnp.float32)
        row_sum = jnp.sum(wide, axis=1, keepdims=True)
        row_square = jnp.sum(wide * wide, axis=1, keepdims=True)
        centre = row_sum * (1.0 / width)
        scaled = ((wide - centre) * gain[...]).astype(jnp.bfloat16)
        flipped = []
        for at in range(0, SPAN, 128):
            count = min(128, SPAN - at)
            column = jnp.where(
                lane[:count] == 0,
                row_sum[at : at + count],
                jnp.where(lane[:count] == 1, row_square[at : at + count], 0.0),
            )
            if count < 128:
                column = jnp.concatenate(
                    [column, jnp.zeros((128 - count, 128), jnp.float32)], axis=0
                )
            flipped.append(jnp.transpose(column)[:TAIL])
        flipped = jnp.concatenate(flipped, axis=1)
        for half, at in halves:
            affine_sum = affine_sums[half]
            part[0:SPAN, at : at + cols] = (
                jnp.dot(scaled, weights[half][...], preferred_element_type=jnp.float32)
                + centre * affine_sum[2:3]
            )
            tail = jnp.where(
                jnp.logical_or(tail_row == 2, tail_row == 3), affine_sum[0:TAIL], 0.0
            )
            part[SPAN : SPAN + TAIL, at : at + cols] = tail
            part[SPAN : SPAN + TAIL, at : at + 256] = jnp.where(
                tail_row[:, :256] < 2, flipped, tail[:, :256]
            )

    for k in (0, 4):
        for half in range(2):

            @pl.when(core == half)
            def _():
                project(parts[k], 4 - k, ((half, 0),))

    for k in (1, 2, 3):
        project(parts[k], 4 - k, ((0, 0), (1, cols)))


def project_rows(counts, hidden, hidden_other, gain, bias, key_weight, value_weight):
    width = hidden.shape[1]
    cols = key_weight.shape[1]
    vmem = pl.BlockSpec(memory_space=pltpu.VMEM)
    hbm = pl.BlockSpec(memory_space=pl.ANY)
    return pl.pallas_call(
        projection_kernel,
        out_shape=[
            jax.ShapeDtypeStruct((SPAN + TAIL, n * cols), jnp.float32) for n in (1, 2, 2, 2, 1)
        ],
        in_specs=[pl.BlockSpec(memory_space=pltpu.SMEM), hbm, hbm] + [vmem] * 4,
        out_specs=[vmem] * 5,
        scratch_shapes=[
            pltpu.VMEM((MOST_UNITS * UNIT, width), jnp.bfloat16),
            pltpu.SemaphoreType.DMA((2, hidden.shape[0] // UNIT)),
        ],
        compiler_params=pltpu.CompilerParams(vmem_limit_bytes=40 * MIB),
        cost_estimate=pl.CostEstimate(
            flops=8 * SPAN * width * 2 * cols, bytes_accessed=12 * MIB, transcendentals=0
        ),
    )(counts, hidden, hidden_other, gain, bias, key_weight, value_weight)


def attention_kernel(begin, end, pair_count, *refs):
    refs = list(refs)
    if end:
        lengths = refs.pop(0)
    q = refs.pop(0)
    if begin:
        own_k, own_v = refs.pop(0), refs.pop(0)
    else:
        state = refs.pop(0)
    blocks = refs[: 4 * pair_count]
    out = refs[-1]
    requests, positions, _ = q.shape
    rows = requests * positions
    rate = math.log2(math.e) / math.sqrt(HD)
    first_core = lax.rem(lax.axis_index("store"), 2) == 0

    def scores_of(queries, block):
        return lax.dot_general(
            queries, block, (((1,), (1,)), ((), ())), preferred_element_type=jnp.float32
        )

    def weigh(scores, top, block):
        weights = jnp.exp2((scores - top) * rate).astype(jnp.bfloat16)
        both = jnp.concatenate([block, jnp.ones(block.shape, jnp.bfloat16)], axis=1)
        return jnp.dot(weights, both, preferred_element_type=jnp.float32)

    if begin:
        row = lax.broadcasted_iota(jnp.int32, (positions, positions), 0)
        column = lax.broadcasted_iota(jnp.int32, (positions, positions), 1)
        tops, sums = [], []
        for r in range(requests):
            scores = jnp.where(column <= row, scores_of(q[r], own_k[r]), -jnp.inf)
            top = jnp.max(scores, axis=1, keepdims=True)
            tops.append(top)
            sums.append(weigh(scores, top, own_v[r]))
        top = jnp.concatenate(tops, axis=0)
        total = jnp.concatenate(sums, axis=0)
    else:
        right = state[0, :, HD:]
        top = right[:, HD // 2 : HD // 2 + 1]
        total = jnp.concatenate(
            [state[0, :, :HD], jnp.broadcast_to(right[:, 0:1], (rows, HD))], axis=1
        )
    queries = q[...].reshape(rows, HD)

    def pick(i):
        return jnp.where(first_core, blocks[2 * i][...], blocks[2 * i + 1][...])

    for i in range(pair_count):
        scores = scores_of(queries, pick(2 * i))
        top_next = jnp.maximum(top, jnp.max(scores, axis=1, keepdims=True))
        factor = jnp.exp2((top - top_next) * rate)
        total = total * factor + weigh(scores, top_next, pick(2 * i + 1))
        top = top_next
    if end:
        result = total[:, :HD] / total[:, HD:]
        place = lax.broadcasted_iota(jnp.int32, (positions, HD), 0)
        for r in range(requests):
            part = result[r * positions : (r + 1) * positions]
            out[r] = jnp.where(place < lengths[r], part, 0.0).astype(jnp.bfloat16)
    else:
        lane = lax.broadcasted_iota(jnp.int32, (rows, HD), 1)
        out[0, :, :HD] = total[:, :HD]
        out[0, :, HD:] = jnp.where(lane < HD // 2, total[:, HD:], top)


def attend(q, pairs, suffix=None, state=None, lengths=None):
    requests, positions, width = q.shape
    rows = requests * positions
    heads = width // HD
    whole = pl.BlockSpec((requests, positions, HD), lambda h: (0, 0, h))
    carried = pl.BlockSpec((1, rows, 2 * HD), lambda h: (h, 0, 0))
    specs, operands = [], []
    if lengths is not None:
        specs.append(pl.BlockSpec(memory_space=pltpu.SMEM))
        operands.append(lengths)
    specs.append(whole)
    operands.append(q)
    if suffix is not None:
        specs += [whole] * 2
        operands += list(suffix)
    else:
        specs.append(carried)
        operands.append(state)
    key_rows = positions if suffix is not None else 0
    for pair in pairs:
        key_rows += pair[0][0].shape[0]
        for array, at in pair:
            specs.append(pl.BlockSpec((array.shape[0], HD), lambda h, at=at: (0, at + h)))
            operands.append(array)
    if lengths is not None:
        out_shape, out_spec = jax.ShapeDtypeStruct(q.shape, jnp.bfloat16), whole
    else:
        out_shape, out_spec = jax.ShapeDtypeStruct((heads, rows, 2 * HD), jnp.float32), carried
    return pl.pallas_call(
        functools.partial(
            attention_kernel, suffix is not None, lengths is not None, len(pairs)
        ),
        grid=(heads,),
        out_shape=out_shape,
        in_specs=specs,
        out_specs=out_spec,
        compiler_params=pltpu.CompilerParams(vmem_limit_bytes=40 * MIB),
        cost_estimate=pl.CostEstimate(
            flops=4 * rows * key_rows * width,
            bytes_accessed=6 * MIB,
            transcendentals=rows * key_rows * heads,
        ),
    )(*operands)


def per_device(
    hidden,
    row_counts,
    ln_gain,
    ln_bias,
    key_weight,
    value_weight,
    suffix_q,
    suffix_k,
    suffix_v,
    suffix_lengths,
):
    cols = key_weight.shape[1]
    heads = cols // HD
    store = lax.axis_index("store")
    first_core = store % 2 == 0
    stores = lax.axis_size("store")
    ring = lax.axis_size("req")
    depth = ring * key_weight.shape[0]
    around = [
        (s * ring + z, s * ring + (z + (1 if s % 2 == 0 else ring - 1)) % ring)
        for s in range(stores)
        for z in range(ring)
    ]
    across = [(s, s + 1 - 2 * (s % 2)) for s in range(stores)]
    far = [(s, (s + 2) % 4) for s in range(stores)]

    def step(array):
        return lax.ppermute(array, ("store", "req"), around)

    def swap(array):
        return lax.ppermute(array, "store", across)

    def ordered(mine, other):
        return jnp.where(
            first_core,
            jnp.concatenate([mine, other], axis=1),
            jnp.concatenate([other, mine], axis=1),
        )

    parts = project_rows(
        row_counts,
        hidden,
        swap(hidden),
        ln_gain[None, :],
        ln_bias[None, :],
        key_weight,
        value_weight,
    )
    state = attend(suffix_q, [], suffix=(suffix_k, suffix_v))

    moving = step(parts[0])
    moving = parts[1] + ordered(moving, jnp.zeros_like(moving))
    moving = step(moving) + parts[2]
    moving = step(moving) + parts[3]
    moving = step(moving) + ordered(parts[4], jnp.zeros_like(parts[4]))
    left, right = moving[:, :cols], moving[:, cols:]
    total = jnp.where(first_core, left, right) + swap(jnp.where(first_core, right, left))
    mean = total[SPAN, :SPAN] / depth
    var = total[SPAN + 1, :SPAN] / depth - mean * mean
    rows = (total[:SPAN] - mean[:, None] * total[SPAN + 2][None, :]) * lax.rsqrt(var + epsilon)[
        :, None
    ] + total[SPAN + 3][None, :]
    rows = rows.astype(jnp.bfloat16)

    rows_far = lax.ppermute(rows, "store", far)
    pair = lax.dynamic_slice(row_counts, (store // 2 * 2,), (2,))
    shared = (pair[0] + pair[1]) // ring
    mine = jnp.pad(rows, ((0, 256), (0, 0)))
    mine = lax.dynamic_update_slice(mine, rows_far, (shared, 0))[:256]

    other = swap(mine)
    r0 = step(mine)
    x0 = swap(r0)
    r1 = step(ordered(r0, other))
    x1 = swap(r1)
    r2 = step(r1)
    x2 = swap(r2)
    r3 = step(r2)
    x3 = swap(r3)

    def up(k, half):
        arrays = ((r0, x0), (r1, x1), (r2, x2), (r3, x3))[k]
        at = half * heads if k > 0 else 0
        return ((arrays[0], at), (arrays[1], at))

    def down(k, half):
        return up(k, half)[::-1]

    state = attend(
        suffix_q,
        [
            ((mine, 0), (other, 0), (other, 0), (mine, 0)),
            up(0, 0) + up(1, 1),
            down(1, 0) + down(0, 1),
        ],
        state=state,
    )
    state = attend(suffix_q, [up(1, 0) + up(2, 1), down(2, 0) + down(1, 1)], state=state)
    return attend(
        suffix_q,
        [up(2, 0) + up(3, 1), down(3, 0) + down(2, 1), up(3, 0) + down(3, 1)],
        state=state,
        lengths=suffix_lengths,
    )


def solution(mesh):
    in_specs = (
        P("store", "req"),
        P(),
        P("req"),
        P("req"),
        P("req", "tp"),
        P("req", "tp"),
        P(("store", "req"), None, "tp"),
        P(("store", "req"), None, "tp"),
        P(("store", "req"), None, "tp"),
        P(("store", "req")),
    )
    out_specs = P(("store", "req"), None, "tp")
    return jax.shard_map(
        per_device, mesh=mesh, in_specs=in_specs, out_specs=out_specs, check_vma=False
    )
```

```python
import functools
import math

import jax
import jax.numpy as jnp
from jax import lax
from jax.experimental import pallas as pl
from jax.experimental.pallas import tpu as pltpu
from jax.sharding import PartitionSpec as P

HD = 128
UNIT = 128
MOST_UNITS = 14
SPAN = 16 * MOST_UNITS
TAIL = 8
BLOCK = 256
epsilon = 1e-05
RATE = math.log2(math.e) / math.sqrt(HD)
MIB = 1 << 20


def split(x, count=3):
    pieces = []
    for _ in range(count):
        piece = x.astype(jnp.bfloat16)
        pieces.append(piece)
        x = x - piece.astype(jnp.float32)
    return pieces


def projection_kernel(
    counts, hidden, hidden_other, gain, bias, key_weight, value_weight, *rest
):
    first, second, (rows_in, weights, row_semaphores, weight_semaphores) = (
        rest[:5],
        rest[5:8],
        rest[8:],
    )
    store = lax.axis_index("store")
    me = lax.axis_index("req")
    core = lax.rem(store, 2)
    first_count = counts[store - core]
    second_count = counts[store - core + 1]
    share = (first_count + second_count) // 8
    width = hidden.shape[1]
    cols = key_weight.shape[1]

    def weight_copies(act):
        for side, source in enumerate((key_weight, value_weight)):
            act(
                pltpu.make_async_copy(
                    source, weights.at[lax.rem(core + side, 2)], weight_semaphores.at[side]
                )
            )

    def row_copies(act):
        for side, source in enumerate((hidden, hidden_other)):
            lower = lax.rem(core + side, 2) == 0
            count = jnp.where(lower, first_count, second_count)
            base = SPAN + jnp.where(lower, 0, first_count)
            for unit in range(source.shape[0] // UNIT):

                @pl.when(unit * UNIT < count)
                def _():
                    at = pl.multiple_of(base + unit * UNIT, 32)
                    act(
                        pltpu.make_async_copy(
                            source.at[pl.ds(unit * UNIT, UNIT)],
                            rows_in.at[pl.ds(at, UNIT)],
                            row_semaphores.at[side, unit],
                        )
                    )

    weight_copies(lambda copy: copy.start())
    row_copies(lambda copy: copy.start())

    row_id = lax.broadcasted_iota(jnp.int32, (16, width), 0)
    affine = jnp.where(row_id == 2, gain[...], jnp.where(row_id == 3, bias[...], 0.0))
    pieces = split(affine)
    weight_copies(lambda copy: copy.wait())
    affine_sums = [
        sum(
            jnp.dot(piece, weights[half], preferred_element_type=jnp.float32)
            for piece in pieces
        )
        for half in range(2)
    ]
    row_copies(lambda copy: copy.wait())

    tail_row = lax.broadcasted_iota(jnp.int32, (TAIL, cols), 0)
    lane = lax.broadcasted_iota(jnp.int32, (128, 128), 1)

    for k in range(5):
        steps = 4 - k
        target = lax.rem(me + jnp.where(core == 0, steps, 8 - steps), 8)
        start = jnp.where(store < 2, SPAN + target * share, (target + 1) * share)
        wide = rows_in[pl.ds(pl.multiple_of(start, 16), SPAN), :].astype(jnp.float32)
        row_sum = jnp.sum(wide, axis=1, keepdims=True)
        row_square = jnp.sum(wide * wide, axis=1, keepdims=True)
        centre = row_sum * (1.0 / width)
        scaled = ((wide - centre) * gain[...]).astype(jnp.bfloat16)
        flipped = []
        for at in range(0, SPAN, 128):
            count = min(128, SPAN - at)
            column = jnp.where(
                lane[:count] == 0,
                row_sum[at : at + count],
                jnp.where(lane[:count] == 1, row_square[at : at + count], 0.0),
            )
            if count < 128:
                column = jnp.concatenate(
                    [column, jnp.zeros((128 - count, 128), jnp.float32)], axis=0
                )
            flipped.append(jnp.transpose(column)[:TAIL])
        flipped = jnp.concatenate(flipped, axis=1)
        parts = [first[k]] + ([second[k - 1]] if 1 <= k <= 3 else [])
        for part, half in zip(parts, range(2)):
            affine_sum = affine_sums[half]
            part[0:SPAN, :] = (
                jnp.dot(scaled, weights[half], preferred_element_type=jnp.float32)
                + centre * affine_sum[2:3]
            )
            tail = jnp.where(
                jnp.logical_or(tail_row == 2, tail_row == 3), affine_sum[0:TAIL], 0.0
            )
            part[SPAN : SPAN + TAIL, :] = tail
            part[SPAN : SPAN + TAIL, 0:256] = jnp.where(
                tail_row[:, :256] < 2, flipped, tail[:, :256]
            )


def project_rows(counts, hidden, hidden_other, gain, bias, key_weight, value_weight):
    capacity, width = hidden.shape
    cols = key_weight.shape[1]
    vmem = pl.BlockSpec(memory_space=pltpu.VMEM)
    hbm = pl.BlockSpec(memory_space=pl.ANY)
    return pl.pallas_call(
        projection_kernel,
        out_shape=[jax.ShapeDtypeStruct((SPAN + TAIL, cols), jnp.float32)] * 8,
        in_specs=[pl.BlockSpec(memory_space=pltpu.SMEM), hbm, hbm, vmem, vmem, hbm, hbm],
        out_specs=[vmem] * 8,
        scratch_shapes=[
            pltpu.VMEM((SPAN + MOST_UNITS * UNIT, width), jnp.bfloat16),
            pltpu.VMEM((2, width, cols), jnp.bfloat16),
            pltpu.SemaphoreType.DMA((2, capacity // UNIT)),
            pltpu.SemaphoreType.DMA((2,)),
        ],
        compiler_params=pltpu.CompilerParams(vmem_limit_bytes=56 * MIB),
        cost_estimate=pl.CostEstimate(
            flops=8 * SPAN * width * 2 * cols, bytes_accessed=12 * MIB, transcendentals=0
        ),
    )(counts, hidden, hidden_other, gain, bias, key_weight, value_weight)


def pack_shift(top):
    rows = top.shape[0]
    lane = lax.broadcasted_iota(jnp.int32, (rows, HD), 1)
    left = -jnp.broadcast_to(top, (rows, HD))
    packed = jnp.zeros((rows, HD), jnp.float32)
    for i, piece in enumerate(split(left)):
        packed = jnp.where(lane == i, piece.astype(jnp.float32), packed)
    return packed.astype(jnp.bfloat16)


def own_kernel(q, own_k, own_v, out, shift):
    requests, positions, _ = q.shape
    row = lax.broadcasted_iota(jnp.int32, (positions, positions), 0)
    column = lax.broadcasted_iota(jnp.int32, (positions, positions), 1)
    for r in range(requests):
        at = r * positions
        scores = lax.dot_general(
            q[r], own_k[r], (((1,), (1,)), ((), ())), preferred_element_type=jnp.float32
        )
        scores = jnp.where(column <= row, scores, -jnp.inf)
        top = jnp.max(scores, axis=1, keepdims=True)
        weights = jnp.exp2((scores - top) * RATE).astype(jnp.bfloat16)
        both = jnp.concatenate([own_v[r], jnp.ones((positions, HD), jnp.bfloat16)], axis=1)
        out[0, at : at + positions, :] = jnp.dot(
            weights, both, preferred_element_type=jnp.float32
        )
        shift[0, at : at + positions, :] = pack_shift(top)


def stage_kernel(end, pair_count, *refs):
    refs = list(refs)
    lengths = refs.pop(0) if end else None
    q, state, shift = refs[:3]
    blocks = refs[3 : 3 + 4 * pair_count]
    outs = refs[3 + 4 * pair_count :]
    requests, positions, _ = q.shape
    rows = requests * positions
    first_core = lax.rem(lax.axis_index("store"), 2) == 0

    def pick(i):
        return jnp.where(first_core, blocks[2 * i][...], blocks[2 * i + 1][...])

    keys = jnp.concatenate([pick(2 * i) for i in range(pair_count)], axis=0)
    values = jnp.concatenate([pick(2 * i + 1) for i in range(pair_count)], axis=0)
    ones = jnp.ones(keys.shape, jnp.bfloat16)
    keys = jnp.concatenate([keys, ones], axis=1)
    values = jnp.concatenate([values, ones], axis=1)

    def shifted_scores():
        queries = jnp.concatenate([q[...].reshape(rows, HD), shift[0]], axis=1)
        return lax.dot_general(
            queries, keys, (((1,), (1,)), ((), ())), preferred_element_type=jnp.float32
        )

    def weigh(scores):
        weights = jnp.exp2(scores * RATE).astype(jnp.bfloat16)
        return jnp.dot(weights, values, preferred_element_type=jnp.float32)

    def emit(total, packed):
        if end:
            result = total[:, :HD] / total[:, HD:]
            place = lax.broadcasted_iota(jnp.int32, (positions, HD), 0)
            for r in range(requests):
                part = result[r * positions : (r + 1) * positions]
                outs[0][r] = jnp.where(place < lengths[r], part, 0.0).astype(jnp.bfloat16)
        else:
            outs[0][0] = total
            outs[1][0] = packed

    total = state[0] + weigh(shifted_scores())
    emit(total, shift[0])
    largest = jnp.max(jnp.max(total[:, HD:].reshape(rows // 8, 8, HD), axis=0))

    @pl.when(jnp.logical_not(largest < 1e30))
    def _():
        scores = shifted_scores()
        old = -jnp.sum(shift[0].astype(jnp.float32), axis=1, keepdims=True)
        new = old + jnp.maximum(jnp.max(scores, axis=1, keepdims=True), 0.0)
        moved = new - old
        emit(state[0] * jnp.exp2(-moved * RATE) + weigh(scores - moved), pack_shift(new))


def attend_own(q, k, v):
    requests, positions, width = q.shape
    rows = requests * positions
    heads = width // HD
    whole = pl.BlockSpec((requests, positions, HD), lambda h: (0, 0, h))
    return pl.pallas_call(
        own_kernel,
        grid=(heads,),
        out_shape=[
            jax.ShapeDtypeStruct((heads, rows, 2 * HD), jnp.float32),
            jax.ShapeDtypeStruct((heads, rows, HD), jnp.bfloat16),
        ],
        in_specs=[whole] * 3,
        out_specs=[
            pl.BlockSpec((1, rows, 2 * HD), lambda h: (h, 0, 0)),
            pl.BlockSpec((1, rows, HD), lambda h: (h, 0, 0)),
        ],
        compiler_params=pltpu.CompilerParams(vmem_limit_bytes=40 * MIB),
        cost_estimate=pl.CostEstimate(
            flops=4 * rows * positions * width,
            bytes_accessed=6 * MIB,
            transcendentals=rows * positions * heads,
        ),
    )(q, k, v)


def attend(q, state, pairs, lengths=None):
    requests, positions, width = q.shape
    rows = requests * positions
    heads = width // HD
    whole = pl.BlockSpec((requests, positions, HD), lambda h: (0, 0, h))
    carried = [
        pl.BlockSpec((1, rows, 2 * HD), lambda h: (h, 0, 0)),
        pl.BlockSpec((1, rows, HD), lambda h: (h, 0, 0)),
    ]
    blocks = [array for pair in pairs for array in pair]
    specs = [whole] + carried
    specs += [pl.BlockSpec((array.shape[0], HD), lambda h: (0, h)) for array in blocks]
    operands = [q, *state, *blocks]
    if lengths is not None:
        specs = [pl.BlockSpec(memory_space=pltpu.SMEM)] + specs
        operands = [lengths] + operands
        out_shape, out_specs = jax.ShapeDtypeStruct(q.shape, jnp.bfloat16), whole
    else:
        out_shape = [jax.ShapeDtypeStruct(array.shape, array.dtype) for array in state]
        out_specs = carried
    key_rows = BLOCK * len(pairs)
    return pl.pallas_call(
        functools.partial(stage_kernel, lengths is not None, len(pairs)),
        grid=(heads,),
        out_shape=out_shape,
        in_specs=specs,
        out_specs=out_specs,
        compiler_params=pltpu.CompilerParams(vmem_limit_bytes=40 * MIB),
        cost_estimate=pl.CostEstimate(
            flops=4 * rows * key_rows * width,
            bytes_accessed=8 * MIB,
            transcendentals=rows * key_rows * heads,
        ),
    )(*operands)


def per_device(
    hidden,
    row_counts,
    ln_gain,
    ln_bias,
    key_weight,
    value_weight,
    suffix_q,
    suffix_k,
    suffix_v,
    suffix_lengths,
):
    store = lax.axis_index("store")
    stores = lax.axis_size("store")
    ring = lax.axis_size("req")
    depth = ring * key_weight.shape[0]
    around = [
        (s * ring + z, s * ring + (z + (1 if s % 2 == 0 else ring - 1)) % ring)
        for s in range(stores)
        for z in range(ring)
    ]
    across = [(s, s + 1 - 2 * (s % 2)) for s in range(stores)]
    far = [(s, (s + 2) % 4) for s in range(stores)]

    def step(array):
        return lax.ppermute(array, ("store", "req"), around)

    def swap(array):
        return lax.ppermute(array, "store", across)

    parts = project_rows(
        row_counts,
        hidden,
        swap(hidden),
        ln_gain[None, :],
        ln_bias[None, :],
        key_weight,
        value_weight,
    )
    first, second = parts[:5], parts[5:]

    total = step(first[0]) + first[1]
    rest = step(second[0]) + second[1]
    total = step(total) + first[2]
    rest = step(rest) + second[2]
    state = attend_own(suffix_q, suffix_k, suffix_v)
    total, state = lax.optimization_barrier((total, state))
    total = step(total) + first[3]
    rest = step(rest)
    total = step(total) + first[4]
    total = total + swap(rest)
    mean = total[SPAN, :SPAN] / depth
    var = total[SPAN + 1, :SPAN] / depth - mean * mean
    rows = (total[:SPAN] - mean[:, None] * total[SPAN + 2][None, :]) * lax.rsqrt(var + epsilon)[
        :, None
    ] + total[SPAN + 3][None, :]
    rows = rows.astype(jnp.bfloat16)

    rows_far = lax.ppermute(rows, "store", far)
    low = jnp.where(store < 2, rows, rows_far)
    high = jnp.where(store < 2, rows_far, rows)
    low_rows = (row_counts[0] + row_counts[1]) // ring
    mine = jnp.where(
        jnp.arange(BLOCK, dtype=jnp.int32)[:, None] < low_rows,
        jnp.pad(low, ((0, BLOCK - SPAN), (0, 0))),
        jnp.pad(high, ((BLOCK - SPAN, 0), (0, 0))),
    )

    other = swap(mine)
    g1 = step(mine)
    h1 = step(other)
    xg1 = swap(g1)
    g2 = step(g1)
    xh1 = swap(h1)
    h2 = step(h1)
    xg2 = swap(g2)
    g3 = step(g2)
    xh2 = swap(h2)
    h3 = step(h2)

    def upper(g, xg, h, xh):
        return (g, xg, h, xh)

    def lower(g, xg, h, xh):
        return (xh, h, xg, g)

    near = (g1, xg1, h1, xh1)
    state = attend(
        suffix_q, state, [(mine, other, other, mine), upper(*near), lower(*near)]
    )
    g3, state = lax.optimization_barrier((g3, state))
    xg3 = swap(g3)
    g4 = step(g3)
    xh3 = swap(h3)
    near = (g2, xg2, h2, xh2)
    state = attend(suffix_q, state, [upper(*near), lower(*near)])
    g4, state = lax.optimization_barrier((g4, state))
    xg4 = swap(g4)
    near = (g3, xg3, h3, xh3)
    state = attend(suffix_q, state, [upper(*near), lower(*near)])
    return attend(suffix_q, state, [(g4, xg4, xg4, g4)], lengths=suffix_lengths)


def solution(mesh):
    in_specs = (
        P("store", "req"),
        P(),
        P("req"),
        P("req"),
        P("req", "tp"),
        P("req", "tp"),
        P(("store", "req"), None, "tp"),
        P(("store", "req"), None, "tp"),
        P(("store", "req"), None, "tp"),
        P(("store", "req")),
    )
    out_specs = P(("store", "req"), None, "tp")
    return jax.shard_map(
        per_device, mesh=mesh, in_specs=in_specs, out_specs=out_specs, check_vma=False
    )
```

```python
import functools
import math

import jax
import jax.numpy as jnp
from jax import lax
from jax.experimental import pallas as pl
from jax.experimental.pallas import tpu as pltpu
from jax.sharding import PartitionSpec as P

HD = 128
UNIT = 128
MOST_UNITS = 14
SPAN = 16 * MOST_UNITS
TAIL = 8
BLOCK = 256
epsilon = 1e-05
RATE = math.log2(math.e) / math.sqrt(HD)
MIB = 1 << 20


def split(x, count=3):
    pieces = []
    for _ in range(count):
        piece = x.astype(jnp.bfloat16)
        pieces.append(piece)
        x = x - piece.astype(jnp.float32)
    return pieces


def put_message(out, block, tail):
    out[0:SPAN, :] = block.astype(jnp.bfloat16)
    row = lax.broadcasted_iota(jnp.int32, (16, tail.shape[1]), 0)
    packed = jnp.zeros(row.shape, jnp.float32)
    for n, piece in enumerate(split(jnp.concatenate([tail, tail], axis=0))):
        packed = jnp.where(row // 4 == n, piece.astype(jnp.float32), packed)
    out[SPAN : SPAN + 16, :] = packed.astype(jnp.bfloat16)


def message_tail(message):
    pieces = message[SPAN : SPAN + 16, :].astype(jnp.float32)
    tail = pieces[:8] + pieces[8:]
    return tail + jnp.concatenate([tail[4:], tail[:4]], axis=0)


def affine_kernel(counts, hidden, gain, bias, key_weight, value_weight, *outs):
    row = lax.broadcasted_iota(jnp.int32, (16, gain.shape[0]), 0) % 4
    affine = jnp.where(
        row == 2, gain[...][None, :], jnp.where(row == 3, bias[...][None, :], 0.0)
    )
    affine = jnp.concatenate(split(affine), axis=0)
    sums = []
    for weight in (key_weight, value_weight):
        total = jnp.dot(affine, weight[...], preferred_element_type=jnp.float32)
        sums.append(sum(total[16 * n : 16 * n + TAIL] for n in range(3)))
    own_is_first = lax.rem(lax.axis_index("store"), 2) == 0
    outs[0][...] = jnp.where(own_is_first, sums[0], sums[1])
    outs[1][...] = jnp.where(own_is_first, sums[1], sums[0])


def project_affine(counts, hidden, gain, bias, key_weight, value_weight):
    width, cols = key_weight.shape
    vmem = pl.BlockSpec(memory_space=pltpu.VMEM)
    return pl.pallas_call(
        affine_kernel,
        out_shape=[jax.ShapeDtypeStruct((TAIL, cols), jnp.float32)] * 2,
        in_specs=[pl.BlockSpec(memory_space=pltpu.SMEM)] + [vmem] * 5,
        out_specs=[vmem] * 2,
        compiler_params=pltpu.CompilerParams(vmem_limit_bytes=32 * MIB),
        cost_estimate=pl.CostEstimate(
            flops=4 * 48 * width * cols, bytes_accessed=6 * MIB, transcendentals=0
        ),
    )(counts, hidden, gain, bias, key_weight, value_weight)


def projection_kernel(plan, counts, hidden, hidden_other, gain, *rest):
    opening = len(plan) == 2
    given, affine_sums = rest[:2], rest[2:4]
    outs, (rows_in, weights) = list(rest[4:-2]), rest[-2:]
    store = lax.axis_index("store")
    me = lax.axis_index("req")
    core = lax.rem(store, 2)
    first_count = counts[store - core]
    units = (first_count + counts[store - core + 1]) // UNIT
    low = store < 2
    capacity, width = hidden.shape
    cols = weights.shape[2]
    own_is_first = core == 0

    @pl.when(own_is_first)
    def _():
        weights[0] = given[0][...]
        weights[1] = given[1][...]

    @pl.when(jnp.logical_not(own_is_first))
    def _():
        weights[0] = given[1][...]
        weights[1] = given[0][...]

    tail_row = lax.broadcasted_iota(jnp.int32, (TAIL, cols), 0)
    lane = lax.broadcasted_iota(jnp.int32, (SPAN, 128), 1)
    fill = jnp.zeros((256 - SPAN, 128), jnp.float32)
    gains = gain[...][None, :]
    for step, sides in plan:
        target = lax.rem(me + jnp.where(own_is_first, step, 8 - step), 8)
        base = target * units - jnp.where(low, 0, MOST_UNITS - units)
        for g in range(MOST_UNITS):
            row = (base + g) * 16
            in_first = row < first_count
            at = jnp.where(in_first, row, row - first_count)
            at = pl.multiple_of(jnp.clip(at, 0, capacity - 16), 16)
            from_own = in_first == own_is_first
            rows_in[pl.ds(g * 16, 16), :] = jnp.where(
                from_own, hidden[pl.ds(at, 16), :], hidden_other[pl.ds(at, 16), :]
            )
        wide = rows_in[...].astype(jnp.float32)
        row_sum = jnp.sum(wide, axis=1, keepdims=True)
        row_square = jnp.sum(wide * wide, axis=1, keepdims=True)
        centre = row_sum * (1.0 / width)
        left = ((wide - centre) * gains).astype(jnp.bfloat16)
        moments = jnp.concatenate(
            [jnp.where(lane == 0, row_sum, jnp.where(lane == 1, row_square, 0.0)), fill], axis=0
        )
        moments = jnp.concatenate(
            [jnp.transpose(moments[:128])[:TAIL], jnp.transpose(moments[128:])[:TAIL]], axis=1
        )
        moments = jnp.concatenate(
            [moments, jnp.zeros((TAIL, cols - 256), jnp.float32)], axis=1
        )
        for side in sides:
            out = outs.pop(0)
            affine_sum = affine_sums[side][...]
            block = (
                jnp.dot(left, weights[side], preferred_element_type=jnp.float32)
                + centre * affine_sum[2:3]
            )
            tail = jnp.where(tail_row % 4 < 2, moments, affine_sum)
            if opening:
                put_message(out, block, tail)
            else:
                out[0:SPAN, :] = block
                out[SPAN : SPAN + TAIL, :] = tail


def project_rows(plan, counts, *operands):
    capacity, width = operands[0].shape
    cols = operands[3].shape[1]
    vmem = pl.BlockSpec(memory_space=pltpu.VMEM)
    pieces = sum(len(sides) for _, sides in plan)
    if len(plan) == 2:
        outs = [jax.ShapeDtypeStruct((SPAN + 16, cols), jnp.bfloat16)] * pieces
    else:
        outs = [jax.ShapeDtypeStruct((SPAN + TAIL, cols), jnp.float32)] * pieces
    return pl.pallas_call(
        functools.partial(projection_kernel, plan),
        out_shape=outs,
        in_specs=[pl.BlockSpec(memory_space=pltpu.SMEM)] + [vmem] * len(operands),
        out_specs=[vmem] * len(outs),
        scratch_shapes=[
            pltpu.VMEM((SPAN, width), jnp.bfloat16),
            pltpu.VMEM((2, width, cols), jnp.bfloat16),
        ],
        compiler_params=pltpu.CompilerParams(vmem_limit_bytes=32 * MIB),
        cost_estimate=pl.CostEstimate(
            flops=pieces * SPAN * width * 2 * cols, bytes_accessed=4 * MIB, transcendentals=0
        ),
    )(counts, *operands)


def finish_kernel(depth, block, ours, theirs, out):
    total = block[0:SPAN, :]
    tail = block[SPAN : SPAN + TAIL, :]
    for message in (ours, theirs):
        total = total + message[0:SPAN, :].astype(jnp.float32)
        tail = tail + message_tail(message)
    fill = jnp.zeros((128 - TAIL, 128), jnp.float32)
    columns = jnp.concatenate(
        [
            jnp.transpose(jnp.concatenate([tail[:, at : at + 128], fill], axis=0))
            for at in (0, 128)
        ],
        axis=0,
    )[:SPAN]
    mean = columns[:, 0:1] / depth
    var = columns[:, 1:2] / depth - mean * mean
    out[...] = ((total - mean * tail[2:3]) * lax.rsqrt(var + epsilon) + tail[3:4]).astype(
        jnp.bfloat16
    )


def finish(block, ours, theirs, depth):
    vmem = pl.BlockSpec(memory_space=pltpu.VMEM)
    return pl.pallas_call(
        functools.partial(finish_kernel, depth),
        out_shape=jax.ShapeDtypeStruct((SPAN, block.shape[1]), jnp.bfloat16),
        in_specs=[vmem] * 3,
        out_specs=vmem,
        compiler_params=pltpu.CompilerParams(vmem_limit_bytes=16 * MIB),
        cost_estimate=pl.CostEstimate(
            flops=4 * SPAN * block.shape[1], bytes_accessed=2 * MIB, transcendentals=SPAN
        ),
    )(block, ours, theirs)


def merge_kernel(counts, rows, rows_far, out):
    low = lax.axis_index("store") < 2
    live = (counts[0] + counts[1]) // 8
    lower = jnp.where(low, rows[...], rows_far[...])
    higher = jnp.where(low, rows_far[...], rows[...])
    edge = BLOCK - SPAN
    place = lax.broadcasted_iota(jnp.int32, (SPAN - edge, rows.shape[1]), 0) + edge
    out[0:edge, :] = lower[:edge]
    out[edge:SPAN, :] = jnp.where(
        place < live, lower[edge:].astype(jnp.float32), higher[: SPAN - edge].astype(jnp.float32)
    ).astype(jnp.bfloat16)
    out[SPAN:BLOCK, :] = higher[SPAN - edge :]


def merge(counts, rows, rows_far):
    vmem = pl.BlockSpec(memory_space=pltpu.VMEM)
    return pl.pallas_call(
        merge_kernel,
        out_shape=jax.ShapeDtypeStruct((BLOCK, rows.shape[1]), jnp.bfloat16),
        in_specs=[pl.BlockSpec(memory_space=pltpu.SMEM)] + [vmem] * 2,
        out_specs=vmem,
        compiler_params=pltpu.CompilerParams(vmem_limit_bytes=16 * MIB),
        cost_estimate=pl.CostEstimate(
            flops=BLOCK * rows.shape[1], bytes_accessed=MIB, transcendentals=0
        ),
    )(counts, rows, rows_far)


def relay_kernel(received, block, out):
    put_message(
        out,
        received[0:SPAN, :].astype(jnp.float32) + block[0:SPAN, :],
        message_tail(received) + block[SPAN : SPAN + TAIL, :],
    )


def relay(received, block):
    vmem = pl.BlockSpec(memory_space=pltpu.VMEM)
    return pl.pallas_call(
        relay_kernel,
        out_shape=jax.ShapeDtypeStruct(received.shape, received.dtype),
        in_specs=[vmem] * 2,
        out_specs=vmem,
        compiler_params=pltpu.CompilerParams(vmem_limit_bytes=16 * MIB),
        cost_estimate=pl.CostEstimate(
            flops=2 * SPAN * block.shape[1], bytes_accessed=2 * MIB, transcendentals=0
        ),
    )(received, block)


def pack_shift(top):
    rows = top.shape[0]
    lane = lax.broadcasted_iota(jnp.int32, (rows, HD), 1)
    left = -jnp.broadcast_to(top, (rows, HD))
    packed = jnp.zeros((rows, HD), jnp.float32)
    for i, piece in enumerate(split(left)):
        packed = jnp.where(lane == i, piece.astype(jnp.float32), packed)
    return packed.astype(jnp.bfloat16)


def own_kernel(q, own_k, own_v, out, shift):
    requests, positions, width = q.shape
    row = lax.broadcasted_iota(jnp.int32, (positions, positions), 0)
    column = lax.broadcasted_iota(jnp.int32, (positions, positions), 1)
    ones = jnp.ones((positions, HD), jnp.bfloat16)
    for head in range(width // HD):
        columns = slice(head * HD, (head + 1) * HD)
        for r in range(requests):
            at = r * positions
            scores = lax.dot_general(
                q[r, :, columns],
                own_k[r, :, columns],
                (((1,), (1,)), ((), ())),
                preferred_element_type=jnp.float32,
            )
            scores = jnp.where(column <= row, scores, -jnp.inf)
            top = jnp.max(scores, axis=1, keepdims=True)
            weights = jnp.exp2((scores - top) * RATE).astype(jnp.bfloat16)
            both = jnp.concatenate([own_v[r, :, columns], ones], axis=1)
            out[head, at : at + positions, :] = jnp.dot(
                weights, both, preferred_element_type=jnp.float32
            )
            shift[head, at : at + positions, :] = pack_shift(top)


def stage_kernel(end, pair_count, *refs):
    refs = list(refs)
    lengths = refs.pop(0) if end else None
    q, state, shift = refs[:3]
    blocks = refs[3 : 3 + 4 * pair_count]
    outs = refs[3 + 4 * pair_count :]
    requests, positions, width = q.shape
    rows = requests * positions
    heads = width // HD
    first_core = lax.rem(lax.axis_index("store"), 2) == 0
    ones = jnp.ones((BLOCK * pair_count, HD), jnp.bfloat16)

    def pick(first, columns):
        return jnp.concatenate(
            [
                jnp.where(first_core, blocks[i][:, columns], blocks[i + 1][:, columns])
                for i in range(first, 4 * pair_count, 4)
            ],
            axis=0,
        )

    def shifted_scores(head, columns):
        queries = jnp.concatenate([q[:, :, columns].reshape(rows, HD), shift[head]], axis=1)
        keys = jnp.concatenate([pick(0, columns), ones], axis=1)
        return lax.dot_general(
            queries, keys, (((1,), (1,)), ((), ())), preferred_element_type=jnp.float32
        )

    def weigh(scores, columns):
        weights = jnp.exp2(scores * RATE).astype(jnp.bfloat16)
        values = jnp.concatenate([pick(2, columns), ones], axis=1)
        return jnp.dot(weights, values, preferred_element_type=jnp.float32)

    def emit(head, columns, total, packed):
        if end:
            result = total[:, :HD] / total[:, HD:]
            place = lax.broadcasted_iota(jnp.int32, (positions, HD), 0)
            for r in range(requests):
                part = result[r * positions : (r + 1) * positions]
                outs[0][r, :, columns] = jnp.where(place < lengths[r], part, 0.0).astype(
                    jnp.bfloat16
                )
        else:
            outs[0][head] = total
            outs[1][head] = packed

    largest = jnp.zeros((8, HD), jnp.float32)
    for head in range(heads):
        columns = slice(head * HD, (head + 1) * HD)
        total = state[head] + weigh(shifted_scores(head, columns), columns)
        emit(head, columns, total, shift[head])
        largest = jnp.maximum(
            largest, jnp.max(total[:, HD:].reshape(rows // 8, 8, HD), axis=0)
        )

    @pl.when(jnp.logical_not(jnp.max(largest) < 1e30))
    def _():
        def one_head(head, carry):
            columns = pl.ds(pl.multiple_of(head * HD, HD), HD)
            scores = shifted_scores(head, columns)
            old = -jnp.sum(shift[head].astype(jnp.float32), axis=1, keepdims=True)
            new = old + jnp.maximum(jnp.max(scores, axis=1, keepdims=True), 0.0)
            moved = new - old
            total = state[head] * jnp.exp2(-moved * RATE) + weigh(scores - moved, columns)
            emit(head, columns, total, pack_shift(new))
            return carry

        lax.fori_loop(0, heads, one_head, 0)


def attend_own(q, k, v):
    requests, positions, width = q.shape
    rows = requests * positions
    heads = width // HD
    vmem = pl.BlockSpec(memory_space=pltpu.VMEM)
    return pl.pallas_call(
        own_kernel,
        out_shape=[
            jax.ShapeDtypeStruct((heads, rows, 2 * HD), jnp.float32),
            jax.ShapeDtypeStruct((heads, rows, HD), jnp.bfloat16),
        ],
        in_specs=[vmem] * 3,
        out_specs=[vmem] * 2,
        compiler_params=pltpu.CompilerParams(vmem_limit_bytes=32 * MIB),
        cost_estimate=pl.CostEstimate(
            flops=4 * rows * positions * width,
            bytes_accessed=6 * MIB,
            transcendentals=rows * positions * heads,
        ),
    )(q, k, v)


def attend(q, state, pairs, lengths=None):
    requests, positions, width = q.shape
    rows = requests * positions
    vmem = pl.BlockSpec(memory_space=pltpu.VMEM)
    operands = [q, *state] + [array for pair in pairs for array in pair]
    specs = [vmem] * len(operands)
    if lengths is not None:
        specs = [pl.BlockSpec(memory_space=pltpu.SMEM)] + specs
        operands = [lengths] + operands
        out_shape, out_specs = jax.ShapeDtypeStruct(q.shape, jnp.bfloat16), vmem
    else:
        out_shape = [jax.ShapeDtypeStruct(array.shape, array.dtype) for array in state]
        out_specs = [vmem] * 2
    key_rows = BLOCK * len(pairs)
    return pl.pallas_call(
        functools.partial(stage_kernel, lengths is not None, len(pairs)),
        out_shape=out_shape,
        in_specs=specs,
        out_specs=out_specs,
        compiler_params=pltpu.CompilerParams(vmem_limit_bytes=32 * MIB),
        cost_estimate=pl.CostEstimate(
            flops=4 * rows * key_rows * width,
            bytes_accessed=8 * MIB,
            transcendentals=rows * key_rows * width // HD,
        ),
    )(*operands)


def per_device(
    hidden,
    row_counts,
    ln_gain,
    ln_bias,
    key_weight,
    value_weight,
    suffix_q,
    suffix_k,
    suffix_v,
    suffix_lengths,
):
    store = lax.axis_index("store")
    stores = lax.axis_size("store")
    ring = lax.axis_size("req")
    depth = ring * key_weight.shape[0]
    around = [
        (s * ring + z, s * ring + (z + (1 if s % 2 == 0 else ring - 1)) % ring)
        for s in range(stores)
        for z in range(ring)
    ]
    across = [(s, s + 1 - 2 * (s % 2)) for s in range(stores)]
    far = [(s, (s + 2) % 4) for s in range(stores)]

    def step(array):
        return lax.ppermute(array, ("store", "req"), around)

    def swap(array):
        return lax.ppermute(array, "store", across)

    other_hidden = swap(hidden)
    weights = (key_weight, value_weight)
    affine = project_affine(row_counts, hidden, ln_gain, ln_bias, *weights)
    inputs = (row_counts, hidden, other_hidden, ln_gain, *weights, *affine)
    total, rest = project_rows(((4, (0,)), (3, (1,))), *inputs)
    f1, f2, s2, f3, s3, f4 = project_rows(
        ((3, (0,)), (2, (0, 1)), (1, (0, 1)), (0, (0,))), *inputs
    )

    total = relay(step(total), f1)
    rest = relay(step(rest), s2)
    total = relay(step(total), f2)
    rest = relay(step(rest), s3)
    state = attend_own(suffix_q, suffix_k, suffix_v)
    total = step(total)
    total, state = lax.optimization_barrier((total, state))
    total = step(relay(total, f3))
    rows = finish(f4, total, swap(step(rest)), depth)

    mine = merge(row_counts, rows, lax.ppermute(rows, "store", far))

    other = swap(mine)
    g1 = step(mine)
    h1 = step(other)
    xg1 = swap(g1)
    g2 = step(g1)
    xh1 = swap(h1)
    h2 = step(h1)
    xg2 = swap(g2)
    xh2 = swap(h2)
    g3 = step(g2)

    def upper(g, xg, h, xh):
        return (g, xg, h, xh)

    def lower(g, xg, h, xh):
        return (xh, h, xg, g)

    h2, state = lax.optimization_barrier((h2, state))
    h3 = step(h2)
    near = (g1, xg1, h1, xh1)
    state = attend(
        suffix_q, state, [(mine, other, other, mine), upper(*near), lower(*near)]
    )
    g3, state = lax.optimization_barrier((g3, state))
    xg3 = swap(g3)
    g4 = step(g3)
    h3, state = lax.optimization_barrier((h3, state))
    xh3 = swap(h3)
    near = (g2, xg2, h2, xh2)
    state = attend(suffix_q, state, [upper(*near), lower(*near)])
    near = (g3, xg3, h3, xh3)
    state = attend(suffix_q, state, [upper(*near), lower(*near)])
    g4, state = lax.optimization_barrier((g4, state))
    xg4 = swap(g4)
    return attend(suffix_q, state, [(g4, xg4, xg4, g4)], lengths=suffix_lengths)


def solution(mesh):
    in_specs = (
        P("store", "req"),
        P(),
        P("req"),
        P("req"),
        P("req", "tp"),
        P("req", "tp"),
        P(("store", "req"), None, "tp"),
        P(("store", "req"), None, "tp"),
        P(("store", "req"), None, "tp"),
        P(("store", "req")),
    )
    out_specs = P(("store", "req"), None, "tp")
    return jax.shard_map(
        per_device, mesh=mesh, in_specs=in_specs, out_specs=out_specs, check_vma=False
    )
```

```python
import functools
import math

import jax
import jax.numpy as jnp
from jax import lax
from jax.experimental import pallas as pl
from jax.experimental.pallas import tpu as pltpu
from jax.sharding import PartitionSpec as P

HD = 128
UNIT = 128
MOST_UNITS = 14
SPAN = 16 * MOST_UNITS
TAIL = 8
BLOCK = 256
epsilon = 1e-05
RATE = math.log2(math.e) / math.sqrt(HD)
MIB = 1 << 20


def split(x, count=3):
    pieces = []
    for _ in range(count):
        piece = x.astype(jnp.bfloat16)
        pieces.append(piece)
        x = x - piece.astype(jnp.float32)
    return pieces


def put_message(out, block, tail):
    out[0:SPAN, :] = block.astype(jnp.bfloat16)
    row = lax.broadcasted_iota(jnp.int32, (16, tail.shape[1]), 0)
    packed = jnp.zeros(row.shape, jnp.float32)
    for n, piece in enumerate(split(jnp.concatenate([tail, tail], axis=0))):
        packed = jnp.where(row // 4 == n, piece.astype(jnp.float32), packed)
    out[SPAN : SPAN + 16, :] = packed.astype(jnp.bfloat16)


def message_tail(message):
    pieces = message[SPAN : SPAN + 16, :].astype(jnp.float32)
    tail = pieces[:8] + pieces[8:]
    return tail + jnp.concatenate([tail[4:], tail[:4]], axis=0)


def affine_kernel(counts, hidden, gain, bias, key_weight, value_weight, *outs):
    row = lax.broadcasted_iota(jnp.int32, (16, gain.shape[0]), 0) % 4
    affine = jnp.where(
        row == 2, gain[...][None, :], jnp.where(row == 3, bias[...][None, :], 0.0)
    )
    affine = jnp.concatenate(split(affine), axis=0)
    sums = []
    for weight in (key_weight, value_weight):
        total = jnp.dot(affine, weight[...], preferred_element_type=jnp.float32)
        sums.append(sum(total[16 * n : 16 * n + TAIL] for n in range(3)))
    own_is_first = lax.rem(lax.axis_index("store"), 2) == 0
    outs[0][...] = jnp.where(own_is_first, sums[0], sums[1])
    outs[1][...] = jnp.where(own_is_first, sums[1], sums[0])


def project_affine(counts, hidden, gain, bias, key_weight, value_weight):
    width, cols = key_weight.shape
    vmem = pl.BlockSpec(memory_space=pltpu.VMEM)
    return pl.pallas_call(
        affine_kernel,
        out_shape=[jax.ShapeDtypeStruct((TAIL, cols), jnp.float32)] * 2,
        in_specs=[pl.BlockSpec(memory_space=pltpu.SMEM)] + [vmem] * 5,
        out_specs=[vmem] * 2,
        compiler_params=pltpu.CompilerParams(vmem_limit_bytes=32 * MIB),
        cost_estimate=pl.CostEstimate(
            flops=4 * 48 * width * cols, bytes_accessed=6 * MIB, transcendentals=0
        ),
    )(counts, hidden, gain, bias, key_weight, value_weight)


def projection_kernel(plan, counts, hidden, hidden_other, gain, *rest):
    opening = len(plan) == 2
    given, affine_sums = rest[:2], rest[2:4]
    outs, (rows_in, weights) = list(rest[4:-2]), rest[-2:]
    store = lax.axis_index("store")
    me = lax.axis_index("req")
    core = lax.rem(store, 2)
    first_count = counts[store - core]
    units = (first_count + counts[store - core + 1]) // UNIT
    low = store < 2
    capacity, width = hidden.shape
    cols = weights.shape[2]
    own_is_first = core == 0

    @pl.when(own_is_first)
    def _():
        weights[0] = given[0][...]
        weights[1] = given[1][...]

    @pl.when(jnp.logical_not(own_is_first))
    def _():
        weights[0] = given[1][...]
        weights[1] = given[0][...]

    tail_row = lax.broadcasted_iota(jnp.int32, (TAIL, cols), 0)
    lane = lax.broadcasted_iota(jnp.int32, (SPAN, 128), 1)
    fill = jnp.zeros((256 - SPAN, 128), jnp.float32)
    gains = gain[...][None, :]
    for step, sides in plan:
        target = lax.rem(me + jnp.where(own_is_first, step, 8 - step), 8)
        base = target * units - jnp.where(low, 0, MOST_UNITS - units)
        for g in range(MOST_UNITS):
            row = (base + g) * 16
            in_first = row < first_count
            at = jnp.where(in_first, row, row - first_count)
            at = pl.multiple_of(jnp.clip(at, 0, capacity - 16), 16)
            from_own = in_first == own_is_first
            rows_in[pl.ds(g * 16, 16), :] = jnp.where(
                from_own, hidden[pl.ds(at, 16), :], hidden_other[pl.ds(at, 16), :]
            )
        wide = rows_in[...].astype(jnp.float32)
        row_sum = jnp.sum(wide, axis=1, keepdims=True)
        row_square = jnp.sum(wide * wide, axis=1, keepdims=True)
        centre = row_sum * (1.0 / width)
        left = ((wide - centre) * gains).astype(jnp.bfloat16)
        moments = jnp.concatenate(
            [jnp.where(lane == 0, row_sum, jnp.where(lane == 1, row_square, 0.0)), fill], axis=0
        )
        moments = jnp.concatenate(
            [jnp.transpose(moments[:128])[:TAIL], jnp.transpose(moments[128:])[:TAIL]], axis=1
        )
        moments = jnp.concatenate(
            [moments, jnp.zeros((TAIL, cols - 256), jnp.float32)], axis=1
        )
        for side in sides:
            out = outs.pop(0)
            affine_sum = affine_sums[side][...]
            block = (
                jnp.dot(left, weights[side], preferred_element_type=jnp.float32)
                + centre * affine_sum[2:3]
            )
            tail = jnp.where(tail_row % 4 < 2, moments, affine_sum)
            if opening:
                put_message(out, block, tail)
            else:
                out[0:SPAN, :] = block
                out[SPAN : SPAN + TAIL, :] = tail


def project_rows(plan, counts, *operands):
    capacity, width = operands[0].shape
    cols = operands[3].shape[1]
    vmem = pl.BlockSpec(memory_space=pltpu.VMEM)
    pieces = sum(len(sides) for _, sides in plan)
    if len(plan) == 2:
        outs = [jax.ShapeDtypeStruct((SPAN + 16, cols), jnp.bfloat16)] * pieces
    else:
        outs = [jax.ShapeDtypeStruct((SPAN + TAIL, cols), jnp.float32)] * pieces
    return pl.pallas_call(
        functools.partial(projection_kernel, plan),
        out_shape=outs,
        in_specs=[pl.BlockSpec(memory_space=pltpu.SMEM)] + [vmem] * len(operands),
        out_specs=[vmem] * len(outs),
        scratch_shapes=[
            pltpu.VMEM((SPAN, width), jnp.bfloat16),
            pltpu.VMEM((2, width, cols), jnp.bfloat16),
        ],
        compiler_params=pltpu.CompilerParams(vmem_limit_bytes=32 * MIB),
        cost_estimate=pl.CostEstimate(
            flops=pieces * SPAN * width * 2 * cols, bytes_accessed=4 * MIB, transcendentals=0
        ),
    )(counts, *operands)


def finish_kernel(depth, block, ours, theirs, out):
    total = block[0:SPAN, :]
    tail = block[SPAN : SPAN + TAIL, :]
    for message in (ours, theirs):
        total = total + message[0:SPAN, :].astype(jnp.float32)
        tail = tail + message_tail(message)
    fill = jnp.zeros((128 - TAIL, 128), jnp.float32)
    columns = jnp.concatenate(
        [
            jnp.transpose(jnp.concatenate([tail[:, at : at + 128], fill], axis=0))
            for at in (0, 128)
        ],
        axis=0,
    )[:SPAN]
    mean = columns[:, 0:1] / depth
    var = columns[:, 1:2] / depth - mean * mean
    out[...] = ((total - mean * tail[2:3]) * lax.rsqrt(var + epsilon) + tail[3:4]).astype(
        jnp.bfloat16
    )


def finish(block, ours, theirs, depth):
    vmem = pl.BlockSpec(memory_space=pltpu.VMEM)
    return pl.pallas_call(
        functools.partial(finish_kernel, depth),
        out_shape=jax.ShapeDtypeStruct((SPAN, block.shape[1]), jnp.bfloat16),
        in_specs=[vmem] * 3,
        out_specs=vmem,
        compiler_params=pltpu.CompilerParams(vmem_limit_bytes=16 * MIB),
        cost_estimate=pl.CostEstimate(
            flops=4 * SPAN * block.shape[1], bytes_accessed=2 * MIB, transcendentals=SPAN
        ),
    )(block, ours, theirs)


def merge_kernel(counts, rows, rows_far, out):
    low = lax.axis_index("store") < 2
    live = (counts[0] + counts[1]) // 8
    lower = jnp.where(low, rows[...], rows_far[...])
    higher = jnp.where(low, rows_far[...], rows[...])
    edge = BLOCK - SPAN
    place = lax.broadcasted_iota(jnp.int32, (SPAN - edge, rows.shape[1]), 0) + edge
    out[0:edge, :] = lower[:edge]
    out[edge:SPAN, :] = jnp.where(
        place < live, lower[edge:].astype(jnp.float32), higher[: SPAN - edge].astype(jnp.float32)
    ).astype(jnp.bfloat16)
    out[SPAN:BLOCK, :] = higher[SPAN - edge :]


def merge(counts, rows, rows_far):
    vmem = pl.BlockSpec(memory_space=pltpu.VMEM)
    return pl.pallas_call(
        merge_kernel,
        out_shape=jax.ShapeDtypeStruct((BLOCK, rows.shape[1]), jnp.bfloat16),
        in_specs=[pl.BlockSpec(memory_space=pltpu.SMEM)] + [vmem] * 2,
        out_specs=vmem,
        compiler_params=pltpu.CompilerParams(vmem_limit_bytes=16 * MIB),
        cost_estimate=pl.CostEstimate(
            flops=BLOCK * rows.shape[1], bytes_accessed=MIB, transcendentals=0
        ),
    )(counts, rows, rows_far)


def relay_kernel(received, block, out):
    put_message(
        out,
        received[0:SPAN, :].astype(jnp.float32) + block[0:SPAN, :],
        message_tail(received) + block[SPAN : SPAN + TAIL, :],
    )


def relay(received, block):
    vmem = pl.BlockSpec(memory_space=pltpu.VMEM)
    return pl.pallas_call(
        relay_kernel,
        out_shape=jax.ShapeDtypeStruct(received.shape, received.dtype),
        in_specs=[vmem] * 2,
        out_specs=vmem,
        compiler_params=pltpu.CompilerParams(vmem_limit_bytes=16 * MIB),
        cost_estimate=pl.CostEstimate(
            flops=2 * SPAN * block.shape[1], bytes_accessed=2 * MIB, transcendentals=0
        ),
    )(received, block)


def pack_shift(top):
    rows = top.shape[0]
    lane = lax.broadcasted_iota(jnp.int32, (rows, HD), 1)
    left = -jnp.broadcast_to(top, (rows, HD))
    packed = jnp.zeros((rows, HD), jnp.float32)
    for i, piece in enumerate(split(left)):
        packed = jnp.where(lane == i, piece.astype(jnp.float32), packed)
    return packed.astype(jnp.bfloat16)


def own_kernel(q, own_k, own_v, out, shift):
    requests, positions, width = q.shape
    row = lax.broadcasted_iota(jnp.int32, (positions, positions), 0)
    column = lax.broadcasted_iota(jnp.int32, (positions, positions), 1)
    ones = jnp.ones((positions, HD), jnp.bfloat16)
    for head in range(width // HD):
        columns = slice(head * HD, (head + 1) * HD)
        for r in range(requests):
            at = r * positions
            scores = lax.dot_general(
                q[r, :, columns],
                own_k[r, :, columns],
                (((1,), (1,)), ((), ())),
                preferred_element_type=jnp.float32,
            )
            scores = jnp.where(column <= row, scores, -jnp.inf)
            top = jnp.max(scores, axis=1, keepdims=True)
            weights = jnp.exp2((scores - top) * RATE).astype(jnp.bfloat16)
            both = jnp.concatenate([own_v[r, :, columns], ones], axis=1)
            out[head, at : at + positions, :] = jnp.dot(
                weights, both, preferred_element_type=jnp.float32
            )
            shift[head, at : at + positions, :] = pack_shift(top)


def stage_kernel(end, pair_count, *refs):
    refs = list(refs)
    lengths = refs.pop(0) if end else None
    q, state, shift = refs[:3]
    blocks = refs[3 : 3 + 4 * pair_count]
    outs = refs[3 + 4 * pair_count :]
    requests, positions, width = q.shape
    rows = requests * positions
    heads = width // HD
    first_core = lax.rem(lax.axis_index("store"), 2) == 0
    ones = jnp.ones((BLOCK * pair_count, HD), jnp.bfloat16)

    def pick(first, columns):
        return jnp.concatenate(
            [
                jnp.where(first_core, blocks[i][:, columns], blocks[i + 1][:, columns])
                for i in range(first, 4 * pair_count, 4)
            ],
            axis=0,
        )

    def shifted_scores(head, columns):
        queries = jnp.concatenate([q[:, :, columns].reshape(rows, HD), shift[head]], axis=1)
        keys = jnp.concatenate([pick(0, columns), ones], axis=1)
        return lax.dot_general(
            queries, keys, (((1,), (1,)), ((), ())), preferred_element_type=jnp.float32
        )

    def weigh(scores, columns):
        weights = jnp.exp2(scores * RATE).astype(jnp.bfloat16)
        values = jnp.concatenate([pick(2, columns), ones], axis=1)
        return jnp.dot(weights, values, preferred_element_type=jnp.float32)

    def emit(head, columns, total, packed):
        if end:
            result = total[:, :HD] / total[:, HD:]
            place = lax.broadcasted_iota(jnp.int32, (positions, HD), 0)
            for r in range(requests):
                part = result[r * positions : (r + 1) * positions]
                outs[0][r, :, columns] = jnp.where(place < lengths[r], part, 0.0).astype(
                    jnp.bfloat16
                )
        else:
            outs[0][head] = total
            outs[1][head] = packed

    largest = jnp.zeros((8, HD), jnp.float32)
    for head in range(heads):
        columns = slice(head * HD, (head + 1) * HD)
        total = state[head] + weigh(shifted_scores(head, columns), columns)
        emit(head, columns, total, shift[head])
        largest = jnp.maximum(
            largest, jnp.max(total[:, HD:].reshape(rows // 8, 8, HD), axis=0)
        )

    @pl.when(jnp.logical_not(jnp.max(largest) < 1e30))
    def _():
        def one_head(head, carry):
            columns = pl.ds(pl.multiple_of(head * HD, HD), HD)
            scores = shifted_scores(head, columns)
            old = -jnp.sum(shift[head].astype(jnp.float32), axis=1, keepdims=True)
            new = old + jnp.maximum(jnp.max(scores, axis=1, keepdims=True), 0.0)
            moved = new - old
            total = state[head] * jnp.exp2(-moved * RATE) + weigh(scores - moved, columns)
            emit(head, columns, total, pack_shift(new))
            return carry

        lax.fori_loop(0, heads, one_head, 0)


def attend_own(q, k, v):
    requests, positions, width = q.shape
    rows = requests * positions
    heads = width // HD
    vmem = pl.BlockSpec(memory_space=pltpu.VMEM)
    return pl.pallas_call(
        own_kernel,
        out_shape=[
            jax.ShapeDtypeStruct((heads, rows, 2 * HD), jnp.float32),
            jax.ShapeDtypeStruct((heads, rows, HD), jnp.bfloat16),
        ],
        in_specs=[vmem] * 3,
        out_specs=[vmem] * 2,
        compiler_params=pltpu.CompilerParams(vmem_limit_bytes=32 * MIB),
        cost_estimate=pl.CostEstimate(
            flops=4 * rows * positions * width,
            bytes_accessed=6 * MIB,
            transcendentals=rows * positions * heads,
        ),
    )(q, k, v)


def attend(q, state, pairs, lengths=None):
    requests, positions, width = q.shape
    rows = requests * positions
    vmem = pl.BlockSpec(memory_space=pltpu.VMEM)
    operands = [q, *state] + [array for pair in pairs for array in pair]
    specs = [vmem] * len(operands)
    if lengths is not None:
        specs = [pl.BlockSpec(memory_space=pltpu.SMEM)] + specs
        operands = [lengths] + operands
        out_shape, out_specs = jax.ShapeDtypeStruct(q.shape, jnp.bfloat16), vmem
    else:
        out_shape = [jax.ShapeDtypeStruct(array.shape, array.dtype) for array in state]
        out_specs = [vmem] * 2
    key_rows = BLOCK * len(pairs)
    return pl.pallas_call(
        functools.partial(stage_kernel, lengths is not None, len(pairs)),
        out_shape=out_shape,
        in_specs=specs,
        out_specs=out_specs,
        compiler_params=pltpu.CompilerParams(vmem_limit_bytes=32 * MIB),
        cost_estimate=pl.CostEstimate(
            flops=4 * rows * key_rows * width,
            bytes_accessed=8 * MIB,
            transcendentals=rows * key_rows * width // HD,
        ),
    )(*operands)


def per_device(
    hidden,
    row_counts,
    ln_gain,
    ln_bias,
    key_weight,
    value_weight,
    suffix_q,
    suffix_k,
    suffix_v,
    suffix_lengths,
):
    store = lax.axis_index("store")
    stores = lax.axis_size("store")
    ring = lax.axis_size("req")
    depth = ring * key_weight.shape[0]
    around = [
        (s * ring + z, s * ring + (z + (1 if s % 2 == 0 else ring - 1)) % ring)
        for s in range(stores)
        for z in range(ring)
    ]
    across = [(s, s + 1 - 2 * (s % 2)) for s in range(stores)]
    far = [(s, (s + 2) % 4) for s in range(stores)]

    def step(array):
        return lax.ppermute(array, ("store", "req"), around)

    def swap(array):
        return lax.ppermute(array, "store", across)

    other_hidden = swap(hidden)
    weights = (key_weight, value_weight)
    affine = project_affine(row_counts, hidden, ln_gain, ln_bias, *weights)
    inputs = (row_counts, hidden, other_hidden, ln_gain, *weights, *affine)
    total, rest = project_rows(((4, (0,)), (3, (1,))), *inputs)
    f1, f2, s2, f3, s3, f4 = project_rows(
        ((3, (0,)), (2, (0, 1)), (1, (0, 1)), (0, (0,))), *inputs
    )

    total = relay(step(total), f1)
    rest = relay(step(rest), s2)
    total = relay(step(total), f2)
    rest = relay(step(rest), s3)
    state = attend_own(suffix_q, suffix_k, suffix_v)
    total = step(total)
    total, state = lax.optimization_barrier((total, state))
    total = step(relay(total, f3))
    rows = finish(f4, total, swap(step(rest)), depth)

    mine = merge(row_counts, rows, lax.ppermute(rows, "store", far))

    other = swap(mine)
    g1 = step(mine)
    h1 = step(other)
    xg1 = swap(g1)
    g2 = step(g1)
    xh1 = swap(h1)
    h2 = step(h1)
    xg2 = swap(g2)
    xh2 = swap(h2)
    g3 = step(g2)

    def upper(g, xg, h, xh):
        return (g, xg, h, xh)

    def lower(g, xg, h, xh):
        return (xh, h, xg, g)

    h2, state = lax.optimization_barrier((h2, state))
    h3 = step(h2)
    near = (g1, xg1, h1, xh1)
    state = attend(
        suffix_q, state, [(mine, other, other, mine), upper(*near), lower(*near)]
    )
    g3, state = lax.optimization_barrier((g3, state))
    xg3 = swap(g3)
    g4 = step(g3)
    near = (g2, xg2, h2, xh2)
    state = attend(suffix_q, state, [upper(*near), lower(*near)])
    xh3 = swap(h3)
    g4, state = lax.optimization_barrier((g4, state))
    xg4 = swap(g4)
    near = (g3, xg3, h3, xh3)
    state = attend(suffix_q, state, [upper(*near), lower(*near)])
    return attend(suffix_q, state, [(g4, xg4, xg4, g4)], lengths=suffix_lengths)


def solution(mesh):
    in_specs = (
        P("store", "req"),
        P(),
        P("req"),
        P("req"),
        P("req", "tp"),
        P("req", "tp"),
        P(("store", "req"), None, "tp"),
        P(("store", "req"), None, "tp"),
        P(("store", "req"), None, "tp"),
        P(("store", "req")),
    )
    out_specs = P(("store", "req"), None, "tp")
    return jax.shard_map(
        per_device, mesh=mesh, in_specs=in_specs, out_specs=out_specs, check_vma=False
    )
```

```python
import functools
import math

import jax
import jax.numpy as jnp
from jax import lax
from jax.experimental import pallas as pl
from jax.experimental.pallas import tpu as pltpu
from jax.sharding import PartitionSpec as P

HD = 128
UNIT = 128
MOST_UNITS = 14
SPAN = 16 * MOST_UNITS
TAIL = 8
BLOCK = 256
epsilon = 1e-05
RATE = math.log2(math.e) / math.sqrt(HD)
MIB = 1 << 20


def split(x, count=3):
    pieces = []
    for _ in range(count):
        piece = x.astype(jnp.bfloat16)
        pieces.append(piece)
        x = x - piece.astype(jnp.float32)
    return pieces


def put_message(out, block, tail):
    out[0:SPAN, :] = block.astype(jnp.bfloat16)
    row = lax.broadcasted_iota(jnp.int32, (16, tail.shape[1]), 0)
    packed = jnp.zeros(row.shape, jnp.float32)
    for n, piece in enumerate(split(jnp.concatenate([tail, tail], axis=0))):
        packed = jnp.where(row // 4 == n, piece.astype(jnp.float32), packed)
    out[SPAN : SPAN + 16, :] = packed.astype(jnp.bfloat16)


def message_tail(message):
    pieces = message[SPAN : SPAN + 16, :].astype(jnp.float32)
    tail = pieces[:8] + pieces[8:]
    return tail + jnp.concatenate([tail[4:], tail[:4]], axis=0)


def affine_kernel(counts, hidden, gain, bias, out):
    row = lax.broadcasted_iota(jnp.int32, (16, gain.shape[0]), 0) % 4
    affine = jnp.where(
        row == 2, gain[...][None, :], jnp.where(row == 3, bias[...][None, :], 0.0)
    )
    for n, piece in enumerate(split(affine)):
        out[16 * n : 16 * (n + 1), :] = piece


def affine_rows(counts, hidden, gain, bias):
    vmem = pl.BlockSpec(memory_space=pltpu.VMEM)
    return pl.pallas_call(
        affine_kernel,
        out_shape=jax.ShapeDtypeStruct((48, gain.shape[0]), jnp.bfloat16),
        in_specs=[pl.BlockSpec(memory_space=pltpu.SMEM)] + [vmem] * 3,
        out_specs=vmem,
        compiler_params=pltpu.CompilerParams(vmem_limit_bytes=32 * MIB),
        cost_estimate=pl.CostEstimate(
            flops=48 * gain.shape[0], bytes_accessed=6 * MIB, transcendentals=0
        ),
    )(counts, hidden, gain, bias)


def window(counts, hidden, hidden_other, step, rows_in):
    store = lax.axis_index("store")
    core = lax.rem(store, 2)
    first_count = counts[store - core]
    units = (first_count + counts[store - core + 1]) // UNIT
    own_is_first = core == 0
    target = lax.rem(
        lax.axis_index("req") + jnp.where(own_is_first, step, 8 - step), 8
    )
    base = target * units - jnp.where(store < 2, 0, MOST_UNITS - units)
    for g in range(MOST_UNITS):
        row = (base + g) * 16
        in_first = row < first_count
        at = jnp.where(in_first, row, row - first_count)
        at = pl.multiple_of(jnp.clip(at, 0, hidden.shape[0] - 16), 16)
        from_own = in_first == own_is_first
        rows_in[pl.ds(g * 16, 16), :] = jnp.where(
            from_own, hidden[pl.ds(at, 16), :], hidden_other[pl.ds(at, 16), :]
        )


def centred(rows_in, gain, cols):
    wide = rows_in[...].astype(jnp.float32)
    row_sum = jnp.sum(wide, axis=1, keepdims=True)
    row_square = jnp.sum(wide * wide, axis=1, keepdims=True)
    centre = row_sum * (1.0 / wide.shape[1])
    left = ((wide - centre) * gain[...][None, :]).astype(jnp.bfloat16)
    lane = lax.broadcasted_iota(jnp.int32, (SPAN, 128), 1) % 4
    fill = jnp.zeros((256 - SPAN, 128), jnp.float32)
    moments = jnp.concatenate(
        [jnp.where(lane == 0, row_sum, jnp.where(lane == 1, row_square, 0.0)), fill], axis=0
    )
    moments = jnp.concatenate(
        [jnp.transpose(moments[:128])[:TAIL], jnp.transpose(moments[128:])[:TAIL]], axis=1
    )
    moments = jnp.concatenate([moments, jnp.zeros((TAIL, cols - 256), jnp.float32)], axis=1)
    return left, centre, moments


def opening_kernel(
    step,
    side,
    counts,
    hidden,
    hidden_other,
    gain,
    affine,
    key_weight,
    value_weight,
    out,
    affine_sum,
    rows_in,
):
    cols = key_weight.shape[1]
    window(counts, hidden, hidden_other, step, rows_in)
    left, centre, moments = centred(rows_in, gain, cols)
    left = jnp.concatenate([left, affine[...]], axis=0)

    def project(weight):
        sums = jnp.dot(left, weight[...], preferred_element_type=jnp.float32)
        total = sum(sums[SPAN + 16 * n : SPAN + 16 * n + TAIL] for n in range(3))
        affine_sum[...] = total
        tail_row = lax.broadcasted_iota(jnp.int32, (TAIL, cols), 0) % 4
        put_message(
            out, sums[:SPAN] + centre * total[2:3], jnp.where(tail_row < 2, moments, total)
        )

    keys_here = lax.rem(lax.axis_index("store") + side, 2) == 0
    for wanted, weight in ((True, key_weight), (False, value_weight)):
        pl.when(keys_here == wanted)(functools.partial(project, weight))


def open_chain(step, side, counts, *operands):
    width = operands[0].shape[1]
    cols = operands[-1].shape[1]
    vmem = pl.BlockSpec(memory_space=pltpu.VMEM)
    return pl.pallas_call(
        functools.partial(opening_kernel, step, side),
        out_shape=[
            jax.ShapeDtypeStruct((SPAN + 16, cols), jnp.bfloat16),
            jax.ShapeDtypeStruct((TAIL, cols), jnp.float32),
        ],
        in_specs=[pl.BlockSpec(memory_space=pltpu.SMEM)] + [vmem] * 6,
        out_specs=[vmem] * 2,
        scratch_shapes=[pltpu.VMEM((SPAN, width), jnp.bfloat16)],
        compiler_params=pltpu.CompilerParams(vmem_limit_bytes=32 * MIB),
        cost_estimate=pl.CostEstimate(
            flops=2 * SPAN * width * cols, bytes_accessed=4 * MIB, transcendentals=0
        ),
    )(counts, *operands)


def projection_kernel(plan, counts, hidden, hidden_other, gain, *rest):
    given, affine_sums = rest[:2], rest[2:4]
    outs, (rows_in, weights) = list(rest[4:-2]), rest[-2:]
    cols = weights.shape[2]
    own_is_first = lax.rem(lax.axis_index("store"), 2) == 0
    for wanted in (True, False):

        @pl.when(own_is_first == wanted)
        def _():
            weights[0] = given[0 if wanted else 1][...]
            weights[1] = given[1 if wanted else 0][...]

    tail_row = lax.broadcasted_iota(jnp.int32, (TAIL, cols), 0) % 4
    for step, sides in plan:
        window(counts, hidden, hidden_other, step, rows_in)
        left, centre, moments = centred(rows_in, gain, cols)
        for side in sides:
            out = outs.pop(0)
            total = affine_sums[side][...]
            out[0:SPAN, :] = (
                jnp.dot(left, weights[side], preferred_element_type=jnp.float32)
                + centre * total[2:3]
            )
            out[SPAN : SPAN + TAIL, :] = jnp.where(tail_row < 2, moments, total)


def project_rows(plan, counts, *operands):
    width = operands[0].shape[1]
    cols = operands[-1].shape[1]
    vmem = pl.BlockSpec(memory_space=pltpu.VMEM)
    pieces = sum(len(sides) for _, sides in plan)
    return pl.pallas_call(
        functools.partial(projection_kernel, plan),
        out_shape=[jax.ShapeDtypeStruct((SPAN + TAIL, cols), jnp.float32)] * pieces,
        in_specs=[pl.BlockSpec(memory_space=pltpu.SMEM)] + [vmem] * len(operands),
        out_specs=[vmem] * pieces,
        scratch_shapes=[
            pltpu.VMEM((SPAN, width), jnp.bfloat16),
            pltpu.VMEM((2, width, cols), jnp.bfloat16),
        ],
        compiler_params=pltpu.CompilerParams(vmem_limit_bytes=32 * MIB),
        cost_estimate=pl.CostEstimate(
            flops=pieces * SPAN * width * 2 * cols, bytes_accessed=4 * MIB, transcendentals=0
        ),
    )(counts, *operands)


def finish_kernel(depth, block, ours, theirs, out):
    total = block[0:SPAN, :]
    tail = block[SPAN : SPAN + TAIL, :]
    for message in (ours, theirs):
        total = total + message[0:SPAN, :].astype(jnp.float32)
        tail = tail + message_tail(message)
    fill = jnp.zeros((128 - TAIL, 128), jnp.float32)
    columns = jnp.concatenate(
        [
            jnp.transpose(jnp.concatenate([tail[:, at : at + 128], fill], axis=0))
            for at in (0, 128)
        ],
        axis=0,
    )[:SPAN]
    mean = columns[:, 0:1] / depth
    var = columns[:, 1:2] / depth - mean * mean
    out[...] = ((total - mean * tail[2:3]) * lax.rsqrt(var + epsilon) + tail[3:4]).astype(
        jnp.bfloat16
    )


def finish(block, ours, theirs, depth):
    vmem = pl.BlockSpec(memory_space=pltpu.VMEM)
    return pl.pallas_call(
        functools.partial(finish_kernel, depth),
        out_shape=jax.ShapeDtypeStruct((SPAN, block.shape[1]), jnp.bfloat16),
        in_specs=[vmem] * 3,
        out_specs=vmem,
        compiler_params=pltpu.CompilerParams(vmem_limit_bytes=16 * MIB),
        cost_estimate=pl.CostEstimate(
            flops=4 * SPAN * block.shape[1], bytes_accessed=2 * MIB, transcendentals=SPAN
        ),
    )(block, ours, theirs)


def merge_kernel(counts, rows, rows_far, out):
    low = lax.axis_index("store") < 2
    live = (counts[0] + counts[1]) // 8
    lower = jnp.where(low, rows[...], rows_far[...])
    higher = jnp.where(low, rows_far[...], rows[...])
    edge = BLOCK - SPAN
    place = lax.broadcasted_iota(jnp.int32, (SPAN - edge, rows.shape[1]), 0) + edge
    out[0:edge, :] = lower[:edge]
    out[edge:SPAN, :] = jnp.where(
        place < live, lower[edge:].astype(jnp.float32), higher[: SPAN - edge].astype(jnp.float32)
    ).astype(jnp.bfloat16)
    out[SPAN:BLOCK, :] = higher[SPAN - edge :]


def merge(counts, rows, rows_far):
    vmem = pl.BlockSpec(memory_space=pltpu.VMEM)
    return pl.pallas_call(
        merge_kernel,
        out_shape=jax.ShapeDtypeStruct((BLOCK, rows.shape[1]), jnp.bfloat16),
        in_specs=[pl.BlockSpec(memory_space=pltpu.SMEM)] + [vmem] * 2,
        out_specs=vmem,
        compiler_params=pltpu.CompilerParams(vmem_limit_bytes=16 * MIB),
        cost_estimate=pl.CostEstimate(
            flops=BLOCK * rows.shape[1], bytes_accessed=MIB, transcendentals=0
        ),
    )(counts, rows, rows_far)


def relay_kernel(received, block, out):
    put_message(
        out,
        received[0:SPAN, :].astype(jnp.float32) + block[0:SPAN, :],
        message_tail(received) + block[SPAN : SPAN + TAIL, :],
    )


def relay(received, block):
    vmem = pl.BlockSpec(memory_space=pltpu.VMEM)
    return pl.pallas_call(
        relay_kernel,
        out_shape=jax.ShapeDtypeStruct(received.shape, received.dtype),
        in_specs=[vmem] * 2,
        out_specs=vmem,
        compiler_params=pltpu.CompilerParams(vmem_limit_bytes=16 * MIB),
        cost_estimate=pl.CostEstimate(
            flops=2 * SPAN * block.shape[1], bytes_accessed=2 * MIB, transcendentals=0
        ),
    )(received, block)


def pack_shift(top):
    rows = top.shape[0]
    lane = lax.broadcasted_iota(jnp.int32, (rows, HD), 1)
    left = -jnp.broadcast_to(top, (rows, HD))
    packed = jnp.zeros((rows, HD), jnp.float32)
    for i, piece in enumerate(split(left)):
        packed = jnp.where(lane == i, piece.astype(jnp.float32), packed)
    return packed.astype(jnp.bfloat16)


def own_kernel(q, own_k, own_v, out, shift):
    requests, positions, width = q.shape
    row = lax.broadcasted_iota(jnp.int32, (positions, positions), 0)
    column = lax.broadcasted_iota(jnp.int32, (positions, positions), 1)
    ones = jnp.ones((positions, HD), jnp.bfloat16)
    for head in range(width // HD):
        columns = slice(head * HD, (head + 1) * HD)
        for r in range(requests):
            at = r * positions
            scores = lax.dot_general(
                q[r, :, columns],
                own_k[r, :, columns],
                (((1,), (1,)), ((), ())),
                preferred_element_type=jnp.float32,
            )
            scores = jnp.where(column <= row, scores, -jnp.inf)
            top = jnp.max(scores, axis=1, keepdims=True)
            weights = jnp.exp2((scores - top) * RATE).astype(jnp.bfloat16)
            both = jnp.concatenate([own_v[r, :, columns], ones], axis=1)
            out[head, at : at + positions, :] = jnp.dot(
                weights, both, preferred_element_type=jnp.float32
            )
            shift[head, at : at + positions, :] = pack_shift(top)


def stage_kernel(end, pair_count, *refs):
    refs = list(refs)
    lengths = refs.pop(0) if end else None
    q, state, shift = refs[:3]
    blocks = refs[3 : 3 + 4 * pair_count]
    outs = refs[3 + 4 * pair_count :]
    requests, positions, width = q.shape
    rows = requests * positions
    heads = width // HD
    first_core = lax.rem(lax.axis_index("store"), 2) == 0
    ones = jnp.ones((BLOCK * pair_count, HD), jnp.bfloat16)

    def pick(first, columns):
        return jnp.concatenate(
            [
                jnp.where(first_core, blocks[i][:, columns], blocks[i + 1][:, columns])
                for i in range(first, 4 * pair_count, 4)
            ],
            axis=0,
        )

    def shifted_scores(head, columns):
        queries = jnp.concatenate([q[:, :, columns].reshape(rows, HD), shift[head]], axis=1)
        keys = jnp.concatenate([pick(0, columns), ones], axis=1)
        return lax.dot_general(
            queries, keys, (((1,), (1,)), ((), ())), preferred_element_type=jnp.float32
        )

    def weigh(scores, columns):
        weights = jnp.exp2(scores * RATE).astype(jnp.bfloat16)
        values = jnp.concatenate([pick(2, columns), ones], axis=1)
        return jnp.dot(weights, values, preferred_element_type=jnp.float32)

    def emit(head, columns, total, packed):
        if end:
            result = total[:, :HD] / total[:, HD:]
            place = lax.broadcasted_iota(jnp.int32, (positions, HD), 0)
            for r in range(requests):
                part = result[r * positions : (r + 1) * positions]
                outs[0][r, :, columns] = jnp.where(place < lengths[r], part, 0.0).astype(
                    jnp.bfloat16
                )
        else:
            outs[0][head] = total
            outs[1][head] = packed

    largest = jnp.zeros((8, HD), jnp.float32)
    for head in range(heads):
        columns = slice(head * HD, (head + 1) * HD)
        total = state[head] + weigh(shifted_scores(head, columns), columns)
        emit(head, columns, total, shift[head])
        largest = jnp.maximum(
            largest, jnp.max(total[:, HD:].reshape(rows // 8, 8, HD), axis=0)
        )

    @pl.when(jnp.logical_not(jnp.max(largest) < 1e30))
    def _():
        def one_head(head, carry):
            columns = pl.ds(pl.multiple_of(head * HD, HD), HD)
            scores = shifted_scores(head, columns)
            old = -jnp.sum(shift[head].astype(jnp.float32), axis=1, keepdims=True)
            new = old + jnp.maximum(jnp.max(scores, axis=1, keepdims=True), 0.0)
            moved = new - old
            total = state[head] * jnp.exp2(-moved * RATE) + weigh(scores - moved, columns)
            emit(head, columns, total, pack_shift(new))
            return carry

        lax.fori_loop(0, heads, one_head, 0)


def attend_own(q, k, v):
    requests, positions, width = q.shape
    rows = requests * positions
    heads = width // HD
    vmem = pl.BlockSpec(memory_space=pltpu.VMEM)
    return pl.pallas_call(
        own_kernel,
        out_shape=[
            jax.ShapeDtypeStruct((heads, rows, 2 * HD), jnp.float32),
            jax.ShapeDtypeStruct((heads, rows, HD), jnp.bfloat16),
        ],
        in_specs=[vmem] * 3,
        out_specs=[vmem] * 2,
        compiler_params=pltpu.CompilerParams(vmem_limit_bytes=32 * MIB),
        cost_estimate=pl.CostEstimate(
            flops=4 * rows * positions * width,
            bytes_accessed=6 * MIB,
            transcendentals=rows * positions * heads,
        ),
    )(q, k, v)


def attend(q, state, pairs, lengths=None):
    requests, positions, width = q.shape
    rows = requests * positions
    vmem = pl.BlockSpec(memory_space=pltpu.VMEM)
    operands = [q, *state] + [array for pair in pairs for array in pair]
    specs = [vmem] * len(operands)
    if lengths is not None:
        specs = [pl.BlockSpec(memory_space=pltpu.SMEM)] + specs
        operands = [lengths] + operands
        out_shape, out_specs = jax.ShapeDtypeStruct(q.shape, jnp.bfloat16), vmem
    else:
        out_shape = [jax.ShapeDtypeStruct(array.shape, array.dtype) for array in state]
        out_specs = [vmem] * 2
    key_rows = BLOCK * len(pairs)
    return pl.pallas_call(
        functools.partial(stage_kernel, lengths is not None, len(pairs)),
        out_shape=out_shape,
        in_specs=specs,
        out_specs=out_specs,
        compiler_params=pltpu.CompilerParams(vmem_limit_bytes=32 * MIB),
        cost_estimate=pl.CostEstimate(
            flops=4 * rows * key_rows * width,
            bytes_accessed=8 * MIB,
            transcendentals=rows * key_rows * width // HD,
        ),
    )(*operands)


def per_device(
    hidden,
    row_counts,
    ln_gain,
    ln_bias,
    key_weight,
    value_weight,
    suffix_q,
    suffix_k,
    suffix_v,
    suffix_lengths,
):
    store = lax.axis_index("store")
    stores = lax.axis_size("store")
    ring = lax.axis_size("req")
    depth = ring * key_weight.shape[0]
    around = [
        (s * ring + z, s * ring + (z + (1 if s % 2 == 0 else ring - 1)) % ring)
        for s in range(stores)
        for z in range(ring)
    ]
    across = [(s, s + 1 - 2 * (s % 2)) for s in range(stores)]
    far = [(s, (s + 2) % 4) for s in range(stores)]

    def step(array):
        return lax.ppermute(array, ("store", "req"), around)

    def swap(array):
        return lax.ppermute(array, "store", across)

    other_hidden = swap(hidden)
    weights = (key_weight, value_weight)
    affine = affine_rows(row_counts, hidden, ln_gain, ln_bias)
    inputs = (row_counts, hidden, other_hidden, ln_gain)
    total, affine_0 = open_chain(4, 0, *inputs, affine, *weights)
    rest, affine_1 = open_chain(3, 1, *inputs, affine, *weights)
    total = step(total)
    rest = step(rest)
    f1, f2, s2, f3, s3, f4 = project_rows(
        ((3, (0,)), (2, (0, 1)), (1, (0, 1)), (0, (0,))),
        *inputs,
        *weights,
        affine_0,
        affine_1,
    )

    total = relay(total, f1)
    rest = relay(rest, s2)
    total = relay(step(total), f2)
    rest = relay(step(rest), s3)
    total = step(relay(step(total), f3))
    rows = finish(f4, total, swap(step(rest)), depth)

    mine = merge(row_counts, rows, lax.ppermute(rows, "store", far))

    other = swap(mine)
    g1 = step(mine)
    h1 = step(other)
    state = attend_own(suffix_q, suffix_k, suffix_v)
    g1, state = lax.optimization_barrier((g1, state))
    xg1 = swap(g1)
    g2 = step(g1)
    xh1 = swap(h1)
    h2 = step(h1)
    xg2 = swap(g2)
    xh2 = swap(h2)
    g3 = step(g2)

    def upper(g, xg, h, xh):
        return (g, xg, h, xh)

    def lower(g, xg, h, xh):
        return (xh, h, xg, g)

    h2, state = lax.optimization_barrier((h2, state))
    h3 = step(h2)
    near = (g1, xg1, h1, xh1)
    state = attend(
        suffix_q, state, [(mine, other, other, mine), upper(*near), lower(*near)]
    )
    g3, state = lax.optimization_barrier((g3, state))
    xg3 = swap(g3)
    g4 = step(g3)
    near = (g2, xg2, h2, xh2)
    state = attend(suffix_q, state, [upper(*near), lower(*near)])
    xh3 = swap(h3)
    g4, state = lax.optimization_barrier((g4, state))
    xg4 = swap(g4)
    near = (g3, xg3, h3, xh3)
    state = attend(suffix_q, state, [upper(*near), lower(*near)])
    return attend(suffix_q, state, [(g4, xg4, xg4, g4)], lengths=suffix_lengths)


def solution(mesh):
    in_specs = (
        P("store", "req"),
        P(),
        P("req"),
        P("req"),
        P("req", "tp"),
        P("req", "tp"),
        P(("store", "req"), None, "tp"),
        P(("store", "req"), None, "tp"),
        P(("store", "req"), None, "tp"),
        P(("store", "req")),
    )
    out_specs = P(("store", "req"), None, "tp")
    return jax.shard_map(
        per_device, mesh=mesh, in_specs=in_specs, out_specs=out_specs, check_vma=False
    )
```

```python
import functools
import math

import jax
import jax.numpy as jnp
from jax import lax
from jax.experimental import pallas as pl
from jax.experimental.pallas import tpu as pltpu
from jax.sharding import PartitionSpec as P

HD = 128
UNIT = 128
MOST_UNITS = 14
SPAN = 16 * MOST_UNITS
TAIL = 8
BLOCK = 256
epsilon = 1e-05
RATE = math.log2(math.e) / math.sqrt(HD)
MIB = 1 << 20


def split(x, count=3):
    pieces = []
    for _ in range(count):
        piece = x.astype(jnp.bfloat16)
        pieces.append(piece)
        x = x - piece.astype(jnp.float32)
    return pieces


def put_message(out, block, tail):
    out[0:SPAN, :] = block.astype(jnp.bfloat16)
    row = lax.broadcasted_iota(jnp.int32, (16, tail.shape[1]), 0)
    packed = jnp.zeros(row.shape, jnp.float32)
    for n, piece in enumerate(split(jnp.concatenate([tail, tail], axis=0))):
        packed = jnp.where(row // 4 == n, piece.astype(jnp.float32), packed)
    out[SPAN : SPAN + 16, :] = packed.astype(jnp.bfloat16)


def message_tail(message):
    pieces = message[SPAN : SPAN + 16, :].astype(jnp.float32)
    tail = pieces[:8] + pieces[8:]
    return tail + jnp.concatenate([tail[4:], tail[:4]], axis=0)


def affine_kernel(place, *refs):
    vector, previous, out = refs[-3:]
    row = lax.broadcasted_iota(jnp.int32, (16, vector.shape[0]), 0) % 4
    here = jnp.where(row == place, vector[...][None, :], 0.0)
    for n, piece in enumerate(split(here)):
        at = slice(16 * n, 16 * (n + 1))
        out[at, :] = piece if place == 2 else previous[at, :] + piece


def affine_rows(counts, hidden, gain, bias):
    vmem = pl.BlockSpec(memory_space=pltpu.VMEM)

    def call(place, *operands):
        return pl.pallas_call(
            functools.partial(affine_kernel, place),
            out_shape=jax.ShapeDtypeStruct((48, gain.shape[0]), jnp.bfloat16),
            in_specs=[pl.BlockSpec(memory_space=pltpu.SMEM)] + [vmem] * (len(operands) - 1),
            out_specs=vmem,
            compiler_params=pltpu.CompilerParams(vmem_limit_bytes=32 * MIB),
            cost_estimate=pl.CostEstimate(
                flops=48 * gain.shape[0], bytes_accessed=6 * MIB, transcendentals=0
            ),
        )(*operands)

    return call(3, counts, hidden, gain, bias, call(2, counts, hidden, gain, hidden))


def window(counts, hidden, hidden_other, step, rows_in):
    store = lax.axis_index("store")
    core = lax.rem(store, 2)
    first_count = counts[store - core]
    units = (first_count + counts[store - core + 1]) // UNIT
    own_is_first = core == 0
    target = lax.rem(
        lax.axis_index("req") + jnp.where(own_is_first, step, 8 - step), 8
    )
    base = target * units - jnp.where(store < 2, 0, MOST_UNITS - units)
    for g in range(MOST_UNITS):
        row = (base + g) * 16
        in_first = row < first_count
        at = jnp.where(in_first, row, row - first_count)
        at = pl.multiple_of(jnp.clip(at, 0, hidden.shape[0] - 16), 16)
        from_own = in_first == own_is_first
        rows_in[pl.ds(g * 16, 16), :] = jnp.where(
            from_own, hidden[pl.ds(at, 16), :], hidden_other[pl.ds(at, 16), :]
        )


def centred(rows_in, gain, cols):
    wide = rows_in[...].astype(jnp.float32)
    row_sum = jnp.sum(wide, axis=1, keepdims=True)
    row_square = jnp.sum(wide * wide, axis=1, keepdims=True)
    centre = row_sum * (1.0 / wide.shape[1])
    left = ((wide - centre) * gain[...][None, :]).astype(jnp.bfloat16)
    lane = lax.broadcasted_iota(jnp.int32, (SPAN, 128), 1) % 4
    fill = jnp.zeros((256 - SPAN, 128), jnp.float32)
    moments = jnp.concatenate(
        [jnp.where(lane == 0, row_sum, jnp.where(lane == 1, row_square, 0.0)), fill], axis=0
    )
    moments = jnp.concatenate(
        [jnp.transpose(moments[:128])[:TAIL], jnp.transpose(moments[128:])[:TAIL]], axis=1
    )
    moments = jnp.concatenate([moments, jnp.zeros((TAIL, cols - 256), jnp.float32)], axis=1)
    return left, centre, moments


def opening_kernel(
    step,
    side,
    counts,
    hidden,
    hidden_other,
    gain,
    affine,
    key_weight,
    value_weight,
    out,
    affine_sum,
    rows_in,
):
    cols = key_weight.shape[1]
    window(counts, hidden, hidden_other, step, rows_in)
    left, centre, moments = centred(rows_in, gain, cols)
    left = jnp.concatenate([left, affine[...]], axis=0)

    def project(weight):
        sums = jnp.dot(left, weight[...], preferred_element_type=jnp.float32)
        total = sum(sums[SPAN + 16 * n : SPAN + 16 * n + TAIL] for n in range(3))
        affine_sum[...] = total
        tail_row = lax.broadcasted_iota(jnp.int32, (TAIL, cols), 0) % 4
        put_message(
            out, sums[:SPAN] + centre * total[2:3], jnp.where(tail_row < 2, moments, total)
        )

    keys_here = lax.rem(lax.axis_index("store") + side, 2) == 0
    for wanted, weight in ((True, key_weight), (False, value_weight)):
        pl.when(keys_here == wanted)(functools.partial(project, weight))


def open_chain(step, side, counts, *operands):
    width = operands[0].shape[1]
    cols = operands[-1].shape[1]
    vmem = pl.BlockSpec(memory_space=pltpu.VMEM)
    return pl.pallas_call(
        functools.partial(opening_kernel, step, side),
        out_shape=[
            jax.ShapeDtypeStruct((SPAN + 16, cols), jnp.bfloat16),
            jax.ShapeDtypeStruct((TAIL, cols), jnp.float32),
        ],
        in_specs=[pl.BlockSpec(memory_space=pltpu.SMEM)] + [vmem] * 6,
        out_specs=[vmem] * 2,
        scratch_shapes=[pltpu.VMEM((SPAN, width), jnp.bfloat16)],
        compiler_params=pltpu.CompilerParams(vmem_limit_bytes=32 * MIB),
        cost_estimate=pl.CostEstimate(
            flops=2 * SPAN * width * cols, bytes_accessed=4 * MIB, transcendentals=0
        ),
    )(counts, *operands)


def projection_kernel(plan, counts, hidden, hidden_other, gain, *rest):
    given, affine_sums = rest[:2], rest[2:4]
    outs, (rows_in, weights) = list(rest[4:-2]), rest[-2:]
    cols = weights.shape[2]
    own_is_first = lax.rem(lax.axis_index("store"), 2) == 0
    for wanted in (True, False):

        @pl.when(own_is_first == wanted)
        def _():
            weights[0] = given[0 if wanted else 1][...]
            weights[1] = given[1 if wanted else 0][...]

    tail_row = lax.broadcasted_iota(jnp.int32, (TAIL, cols), 0) % 4
    for step, sides in plan:
        window(counts, hidden, hidden_other, step, rows_in)
        left, centre, moments = centred(rows_in, gain, cols)
        for side in sides:
            out = outs.pop(0)
            total = affine_sums[side][...]
            out[0:SPAN, :] = (
                jnp.dot(left, weights[side], preferred_element_type=jnp.float32)
                + centre * total[2:3]
            )
            out[SPAN : SPAN + TAIL, :] = jnp.where(tail_row < 2, moments, total)


def project_rows(plan, counts, *operands):
    width = operands[0].shape[1]
    cols = operands[-1].shape[1]
    vmem = pl.BlockSpec(memory_space=pltpu.VMEM)
    pieces = sum(len(sides) for _, sides in plan)
    return pl.pallas_call(
        functools.partial(projection_kernel, plan),
        out_shape=[jax.ShapeDtypeStruct((SPAN + TAIL, cols), jnp.float32)] * pieces,
        in_specs=[pl.BlockSpec(memory_space=pltpu.SMEM)] + [vmem] * len(operands),
        out_specs=[vmem] * pieces,
        scratch_shapes=[
            pltpu.VMEM((SPAN, width), jnp.bfloat16),
            pltpu.VMEM((2, width, cols), jnp.bfloat16),
        ],
        compiler_params=pltpu.CompilerParams(vmem_limit_bytes=32 * MIB),
        cost_estimate=pl.CostEstimate(
            flops=pieces * SPAN * width * 2 * cols, bytes_accessed=4 * MIB, transcendentals=0
        ),
    )(counts, *operands)


def finish_kernel(depth, block, ours, theirs, out):
    total = block[0:SPAN, :]
    tail = block[SPAN : SPAN + TAIL, :]
    for message in (ours, theirs):
        total = total + message[0:SPAN, :].astype(jnp.float32)
        tail = tail + message_tail(message)
    fill = jnp.zeros((128 - TAIL, 128), jnp.float32)
    columns = jnp.concatenate(
        [
            jnp.transpose(jnp.concatenate([tail[:, at : at + 128], fill], axis=0))
            for at in (0, 128)
        ],
        axis=0,
    )[:SPAN]
    mean = columns[:, 0:1] / depth
    var = columns[:, 1:2] / depth - mean * mean
    out[...] = ((total - mean * tail[2:3]) * lax.rsqrt(var + epsilon) + tail[3:4]).astype(
        jnp.bfloat16
    )


def finish(block, ours, theirs, depth):
    vmem = pl.BlockSpec(memory_space=pltpu.VMEM)
    return pl.pallas_call(
        functools.partial(finish_kernel, depth),
        out_shape=jax.ShapeDtypeStruct((SPAN, block.shape[1]), jnp.bfloat16),
        in_specs=[vmem] * 3,
        out_specs=vmem,
        compiler_params=pltpu.CompilerParams(vmem_limit_bytes=16 * MIB),
        cost_estimate=pl.CostEstimate(
            flops=4 * SPAN * block.shape[1], bytes_accessed=2 * MIB, transcendentals=SPAN
        ),
    )(block, ours, theirs)


def merge_kernel(counts, rows, rows_far, out):
    low = lax.axis_index("store") < 2
    live = (counts[0] + counts[1]) // 8
    lower = jnp.where(low, rows[...], rows_far[...])
    higher = jnp.where(low, rows_far[...], rows[...])
    edge = BLOCK - SPAN
    place = lax.broadcasted_iota(jnp.int32, (SPAN - edge, rows.shape[1]), 0) + edge
    out[0:edge, :] = lower[:edge]
    out[edge:SPAN, :] = jnp.where(
        place < live, lower[edge:].astype(jnp.float32), higher[: SPAN - edge].astype(jnp.float32)
    ).astype(jnp.bfloat16)
    out[SPAN:BLOCK, :] = higher[SPAN - edge :]


def merge(counts, rows, rows_far):
    vmem = pl.BlockSpec(memory_space=pltpu.VMEM)
    return pl.pallas_call(
        merge_kernel,
        out_shape=jax.ShapeDtypeStruct((BLOCK, rows.shape[1]), jnp.bfloat16),
        in_specs=[pl.BlockSpec(memory_space=pltpu.SMEM)] + [vmem] * 2,
        out_specs=vmem,
        compiler_params=pltpu.CompilerParams(vmem_limit_bytes=16 * MIB),
        cost_estimate=pl.CostEstimate(
            flops=BLOCK * rows.shape[1], bytes_accessed=MIB, transcendentals=0
        ),
    )(counts, rows, rows_far)


def relay_kernel(received, block, out):
    put_message(
        out,
        received[0:SPAN, :].astype(jnp.float32) + block[0:SPAN, :],
        message_tail(received) + block[SPAN : SPAN + TAIL, :],
    )


def relay(received, block):
    vmem = pl.BlockSpec(memory_space=pltpu.VMEM)
    return pl.pallas_call(
        relay_kernel,
        out_shape=jax.ShapeDtypeStruct(received.shape, received.dtype),
        in_specs=[vmem] * 2,
        out_specs=vmem,
        compiler_params=pltpu.CompilerParams(vmem_limit_bytes=16 * MIB),
        cost_estimate=pl.CostEstimate(
            flops=2 * SPAN * block.shape[1], bytes_accessed=2 * MIB, transcendentals=0
        ),
    )(received, block)


def pack_shift(top):
    rows = top.shape[0]
    lane = lax.broadcasted_iota(jnp.int32, (rows, HD), 1)
    left = -jnp.broadcast_to(top, (rows, HD))
    packed = jnp.zeros((rows, HD), jnp.float32)
    for i, piece in enumerate(split(left)):
        packed = jnp.where(lane == i, piece.astype(jnp.float32), packed)
    return packed.astype(jnp.bfloat16)


def own_kernel(q, own_k, own_v, out, shift):
    requests, positions, width = q.shape
    row = lax.broadcasted_iota(jnp.int32, (positions, positions), 0)
    column = lax.broadcasted_iota(jnp.int32, (positions, positions), 1)
    ones = jnp.ones((positions, HD), jnp.bfloat16)
    for head in range(width // HD):
        columns = slice(head * HD, (head + 1) * HD)
        for r in range(requests):
            at = r * positions
            scores = lax.dot_general(
                q[r, :, columns],
                own_k[r, :, columns],
                (((1,), (1,)), ((), ())),
                preferred_element_type=jnp.float32,
            )
            scores = jnp.where(column <= row, scores, -jnp.inf)
            top = jnp.max(scores, axis=1, keepdims=True)
            weights = jnp.exp2((scores - top) * RATE).astype(jnp.bfloat16)
            both = jnp.concatenate([own_v[r, :, columns], ones], axis=1)
            out[head, at : at + positions, :] = jnp.dot(
                weights, both, preferred_element_type=jnp.float32
            )
            shift[head, at : at + positions, :] = pack_shift(top)


def stage_kernel(end, pair_count, *refs):
    refs = list(refs)
    lengths = refs.pop(0) if end else None
    q, state, shift = refs[:3]
    blocks = refs[3 : 3 + 4 * pair_count]
    outs = refs[3 + 4 * pair_count :]
    requests, positions, width = q.shape
    rows = requests * positions
    heads = width // HD
    first_core = lax.rem(lax.axis_index("store"), 2) == 0
    ones = jnp.ones((BLOCK * pair_count, HD), jnp.bfloat16)

    def pick(first, columns):
        return jnp.concatenate(
            [
                jnp.where(first_core, blocks[i][:, columns], blocks[i + 1][:, columns])
                for i in range(first, 4 * pair_count, 4)
            ],
            axis=0,
        )

    def shifted_scores(head, columns):
        queries = jnp.concatenate([q[:, :, columns].reshape(rows, HD), shift[head]], axis=1)
        keys = jnp.concatenate([pick(0, columns), ones], axis=1)
        return lax.dot_general(
            queries, keys, (((1,), (1,)), ((), ())), preferred_element_type=jnp.float32
        )

    def weigh(scores, columns):
        weights = jnp.exp2(scores * RATE).astype(jnp.bfloat16)
        values = jnp.concatenate([pick(2, columns), ones], axis=1)
        return jnp.dot(weights, values, preferred_element_type=jnp.float32)

    def emit(head, columns, total, packed):
        if end:
            result = total[:, :HD] / total[:, HD:]
            place = lax.broadcasted_iota(jnp.int32, (positions, HD), 0)
            for r in range(requests):
                part = result[r * positions : (r + 1) * positions]
                outs[0][r, :, columns] = jnp.where(place < lengths[r], part, 0.0).astype(
                    jnp.bfloat16
                )
        else:
            outs[0][head] = total
            outs[1][head] = packed

    largest = jnp.zeros((8, HD), jnp.float32)
    for head in range(heads):
        columns = slice(head * HD, (head + 1) * HD)
        total = state[head] + weigh(shifted_scores(head, columns), columns)
        emit(head, columns, total, shift[head])
        largest = jnp.maximum(
            largest, jnp.max(total[:, HD:].reshape(rows // 8, 8, HD), axis=0)
        )

    @pl.when(jnp.logical_not(jnp.max(largest) < 1e30))
    def _():
        def one_head(head, carry):
            columns = pl.ds(pl.multiple_of(head * HD, HD), HD)
            scores = shifted_scores(head, columns)
            old = -jnp.sum(shift[head].astype(jnp.float32), axis=1, keepdims=True)
            new = old + jnp.maximum(jnp.max(scores, axis=1, keepdims=True), 0.0)
            moved = new - old
            total = state[head] * jnp.exp2(-moved * RATE) + weigh(scores - moved, columns)
            emit(head, columns, total, pack_shift(new))
            return carry

        lax.fori_loop(0, heads, one_head, 0)


def attend_own(q, k, v):
    requests, positions, width = q.shape
    rows = requests * positions
    heads = width // HD
    vmem = pl.BlockSpec(memory_space=pltpu.VMEM)
    return pl.pallas_call(
        own_kernel,
        out_shape=[
            jax.ShapeDtypeStruct((heads, rows, 2 * HD), jnp.float32),
            jax.ShapeDtypeStruct((heads, rows, HD), jnp.bfloat16),
        ],
        in_specs=[vmem] * 3,
        out_specs=[vmem] * 2,
        compiler_params=pltpu.CompilerParams(vmem_limit_bytes=32 * MIB),
        cost_estimate=pl.CostEstimate(
            flops=4 * rows * positions * width,
            bytes_accessed=6 * MIB,
            transcendentals=rows * positions * heads,
        ),
    )(q, k, v)


def attend(q, state, pairs, lengths=None):
    requests, positions, width = q.shape
    rows = requests * positions
    vmem = pl.BlockSpec(memory_space=pltpu.VMEM)
    operands = [q, *state] + [array for pair in pairs for array in pair]
    specs = [vmem] * len(operands)
    if lengths is not None:
        specs = [pl.BlockSpec(memory_space=pltpu.SMEM)] + specs
        operands = [lengths] + operands
        out_shape, out_specs = jax.ShapeDtypeStruct(q.shape, jnp.bfloat16), vmem
    else:
        out_shape = [jax.ShapeDtypeStruct(array.shape, array.dtype) for array in state]
        out_specs = [vmem] * 2
    key_rows = BLOCK * len(pairs)
    return pl.pallas_call(
        functools.partial(stage_kernel, lengths is not None, len(pairs)),
        out_shape=out_shape,
        in_specs=specs,
        out_specs=out_specs,
        compiler_params=pltpu.CompilerParams(vmem_limit_bytes=32 * MIB),
        cost_estimate=pl.CostEstimate(
            flops=4 * rows * key_rows * width,
            bytes_accessed=8 * MIB,
            transcendentals=rows * key_rows * width // HD,
        ),
    )(*operands)


def per_device(
    hidden,
    row_counts,
    ln_gain,
    ln_bias,
    key_weight,
    value_weight,
    suffix_q,
    suffix_k,
    suffix_v,
    suffix_lengths,
):
    store = lax.axis_index("store")
    stores = lax.axis_size("store")
    ring = lax.axis_size("req")
    depth = ring * key_weight.shape[0]
    around = [
        (s * ring + z, s * ring + (z + (1 if s % 2 == 0 else ring - 1)) % ring)
        for s in range(stores)
        for z in range(ring)
    ]
    across = [(s, s + 1 - 2 * (s % 2)) for s in range(stores)]
    far = [(s, (s + 2) % 4) for s in range(stores)]

    def step(array):
        return lax.ppermute(array, ("store", "req"), around)

    def swap(array):
        return lax.ppermute(array, "store", across)

    other_hidden = swap(hidden)
    weights = (key_weight, value_weight)
    affine = affine_rows(row_counts, hidden, ln_gain, ln_bias)
    inputs = (row_counts, hidden, other_hidden, ln_gain)
    total, affine_0 = open_chain(4, 0, *inputs, affine, *weights)
    rest, affine_1 = open_chain(3, 1, *inputs, affine, *weights)
    total = step(total)
    rest = step(rest)
    f1, f2, s2, f3, s3, f4 = project_rows(
        ((3, (0,)), (2, (0, 1)), (1, (0, 1)), (0, (0,))),
        *inputs,
        *weights,
        affine_0,
        affine_1,
    )

    total = relay(total, f1)
    rest = relay(rest, s2)
    total = relay(step(total), f2)
    rest = relay(step(rest), s3)
    total = step(relay(step(total), f3))
    rows = finish(f4, total, swap(step(rest)), depth)

    mine = merge(row_counts, rows, lax.ppermute(rows, "store", far))

    other = swap(mine)
    g1 = step(mine)
    h1 = step(other)
    state = attend_own(suffix_q, suffix_k, suffix_v)
    g1, state = lax.optimization_barrier((g1, state))
    xg1 = swap(g1)
    g2 = step(g1)
    xh1 = swap(h1)
    h2 = step(h1)
    xg2 = swap(g2)
    xh2 = swap(h2)
    g3 = step(g2)

    def upper(g, xg, h, xh):
        return (g, xg, h, xh)

    def lower(g, xg, h, xh):
        return (xh, h, xg, g)

    h2, state = lax.optimization_barrier((h2, state))
    h3 = step(h2)
    near = (g1, xg1, h1, xh1)
    state = attend(
        suffix_q, state, [(mine, other, other, mine), upper(*near), lower(*near)]
    )
    g3, state = lax.optimization_barrier((g3, state))
    xg3 = swap(g3)
    g4 = step(g3)
    near = (g2, xg2, h2, xh2)
    state = attend(suffix_q, state, [upper(*near), lower(*near)])
    xh3 = swap(h3)
    g4, state = lax.optimization_barrier((g4, state))
    xg4 = swap(g4)
    near = (g3, xg3, h3, xh3)
    state = attend(suffix_q, state, [upper(*near), lower(*near)])
    return attend(suffix_q, state, [(g4, xg4, xg4, g4)], lengths=suffix_lengths)


def solution(mesh):
    in_specs = (
        P("store", "req"),
        P(),
        P("req"),
        P("req"),
        P("req", "tp"),
        P("req", "tp"),
        P(("store", "req"), None, "tp"),
        P(("store", "req"), None, "tp"),
        P(("store", "req"), None, "tp"),
        P(("store", "req")),
    )
    out_specs = P(("store", "req"), None, "tp")
    return jax.shard_map(
        per_device, mesh=mesh, in_specs=in_specs, out_specs=out_specs, check_vma=False
    )
```

```python
import functools
import math

import jax
import jax.numpy as jnp
from jax import lax
from jax.experimental import pallas as pl
from jax.experimental.pallas import tpu as pltpu
from jax.sharding import PartitionSpec as P

HD = 128
UNIT = 128
MOST_UNITS = 14
SPAN = 16 * MOST_UNITS
TAIL = 8
BLOCK = 256
epsilon = 1e-05
RATE = math.log2(math.e) / math.sqrt(HD)
MIB = 1 << 20


def split(x, count=3):
    pieces = []
    for _ in range(count):
        piece = x.astype(jnp.bfloat16)
        pieces.append(piece)
        x = x - piece.astype(jnp.float32)
    return pieces


def put_message(out, block, tail):
    out[0:SPAN, :] = block.astype(jnp.bfloat16)
    row = lax.broadcasted_iota(jnp.int32, (16, tail.shape[1]), 0)
    packed = jnp.zeros(row.shape, jnp.float32)
    for n, piece in enumerate(split(jnp.concatenate([tail, tail], axis=0))):
        packed = jnp.where(row // 4 == n, piece.astype(jnp.float32), packed)
    out[SPAN : SPAN + 16, :] = packed.astype(jnp.bfloat16)


def message_tail(message):
    pieces = message[SPAN : SPAN + 16, :].astype(jnp.float32)
    tail = pieces[:8] + pieces[8:]
    return tail + jnp.concatenate([tail[4:], tail[:4]], axis=0)


def affine_kernel(place, *refs):
    vector, previous, out = refs[-3:]
    row = lax.broadcasted_iota(jnp.int32, (16, vector.shape[0]), 0) % 4
    here = jnp.where(row == place, vector[...][None, :], 0.0)
    for n, piece in enumerate(split(here)):
        at = slice(16 * n, 16 * (n + 1))
        out[at, :] = piece if place == 2 else previous[at, :] + piece


def affine_rows(counts, hidden, gain, bias):
    vmem = pl.BlockSpec(memory_space=pltpu.VMEM)

    def call(place, *operands):
        return pl.pallas_call(
            functools.partial(affine_kernel, place),
            out_shape=jax.ShapeDtypeStruct((48, gain.shape[0]), jnp.bfloat16),
            in_specs=[pl.BlockSpec(memory_space=pltpu.SMEM)] + [vmem] * (len(operands) - 1),
            out_specs=vmem,
            compiler_params=pltpu.CompilerParams(vmem_limit_bytes=32 * MIB),
            cost_estimate=pl.CostEstimate(
                flops=48 * gain.shape[0], bytes_accessed=6 * MIB, transcendentals=0
            ),
        )(*operands)

    return call(3, counts, hidden, gain, bias, call(2, counts, hidden, gain, hidden))


def window(counts, hidden, hidden_other, step, rows_in):
    store = lax.axis_index("store")
    core = lax.rem(store, 2)
    first_count = counts[store - core]
    units = (first_count + counts[store - core + 1]) // UNIT
    own_is_first = core == 0
    target = lax.rem(
        lax.axis_index("req") + jnp.where(own_is_first, step, 8 - step), 8
    )
    base = target * units - jnp.where(store < 2, 0, MOST_UNITS - units)
    for g in range(MOST_UNITS):
        row = (base + g) * 16
        in_first = row < first_count
        at = jnp.where(in_first, row, row - first_count)
        at = pl.multiple_of(jnp.clip(at, 0, hidden.shape[0] - 16), 16)
        from_own = in_first == own_is_first
        rows_in[pl.ds(g * 16, 16), :] = jnp.where(
            from_own, hidden[pl.ds(at, 16), :], hidden_other[pl.ds(at, 16), :]
        )


def centred(rows_in, gain, cols):
    wide = rows_in[...].astype(jnp.float32)
    row_sum = jnp.sum(wide, axis=1, keepdims=True)
    row_square = jnp.sum(wide * wide, axis=1, keepdims=True)
    centre = row_sum * (1.0 / wide.shape[1])
    left = ((wide - centre) * gain[...][None, :]).astype(jnp.bfloat16)
    lane = lax.broadcasted_iota(jnp.int32, (SPAN, 128), 1) % 4
    fill = jnp.zeros((256 - SPAN, 128), jnp.float32)
    moments = jnp.concatenate(
        [jnp.where(lane == 0, row_sum, jnp.where(lane == 1, row_square, 0.0)), fill], axis=0
    )
    moments = jnp.concatenate(
        [jnp.transpose(moments[:128])[:TAIL], jnp.transpose(moments[128:])[:TAIL]], axis=1
    )
    moments = jnp.concatenate([moments, jnp.zeros((TAIL, cols - 256), jnp.float32)], axis=1)
    return left, centre, moments


def opening_kernel(
    step,
    side,
    counts,
    hidden,
    hidden_other,
    gain,
    affine,
    key_weight,
    value_weight,
    out,
    affine_sum,
    rows_in,
):
    cols = key_weight.shape[1]
    window(counts, hidden, hidden_other, step, rows_in)
    left, centre, moments = centred(rows_in, gain, cols)
    left = jnp.concatenate([left, affine[...]], axis=0)

    def project(weight):
        sums = jnp.dot(left, weight[...], preferred_element_type=jnp.float32)
        total = sum(sums[SPAN + 16 * n : SPAN + 16 * n + TAIL] for n in range(3))
        affine_sum[...] = total
        tail_row = lax.broadcasted_iota(jnp.int32, (TAIL, cols), 0) % 4
        put_message(
            out, sums[:SPAN] + centre * total[2:3], jnp.where(tail_row < 2, moments, total)
        )

    keys_here = lax.rem(lax.axis_index("store") + side, 2) == 0
    for wanted, weight in ((True, key_weight), (False, value_weight)):
        pl.when(keys_here == wanted)(functools.partial(project, weight))


def open_chain(step, side, counts, *operands):
    width = operands[0].shape[1]
    cols = operands[-1].shape[1]
    vmem = pl.BlockSpec(memory_space=pltpu.VMEM)
    return pl.pallas_call(
        functools.partial(opening_kernel, step, side),
        out_shape=[
            jax.ShapeDtypeStruct((SPAN + 16, cols), jnp.bfloat16),
            jax.ShapeDtypeStruct((TAIL, cols), jnp.float32),
        ],
        in_specs=[pl.BlockSpec(memory_space=pltpu.SMEM)] + [vmem] * 6,
        out_specs=[vmem] * 2,
        scratch_shapes=[pltpu.VMEM((SPAN, width), jnp.bfloat16)],
        compiler_params=pltpu.CompilerParams(vmem_limit_bytes=32 * MIB),
        cost_estimate=pl.CostEstimate(
            flops=2 * SPAN * width * cols, bytes_accessed=4 * MIB, transcendentals=0
        ),
    )(counts, *operands)


def projection_kernel(plan, counts, hidden, hidden_other, gain, *rest):
    given, affine_sums = rest[:2], rest[2:4]
    outs, (rows_in, weights) = list(rest[4:-2]), rest[-2:]
    cols = weights.shape[2]
    own_is_first = lax.rem(lax.axis_index("store"), 2) == 0
    for wanted in (True, False):

        @pl.when(own_is_first == wanted)
        def _():
            weights[0] = given[0 if wanted else 1][...]
            weights[1] = given[1 if wanted else 0][...]

    tail_row = lax.broadcasted_iota(jnp.int32, (TAIL, cols), 0) % 4
    for step, sides in plan:
        window(counts, hidden, hidden_other, step, rows_in)
        left, centre, moments = centred(rows_in, gain, cols)
        for side in sides:
            out = outs.pop(0)
            total = affine_sums[side][...]
            out[0:SPAN, :] = (
                jnp.dot(left, weights[side], preferred_element_type=jnp.float32)
                + centre * total[2:3]
            )
            out[SPAN : SPAN + TAIL, :] = jnp.where(tail_row < 2, moments, total)


def project_rows(plan, counts, *operands):
    width = operands[0].shape[1]
    cols = operands[-1].shape[1]
    vmem = pl.BlockSpec(memory_space=pltpu.VMEM)
    pieces = sum(len(sides) for _, sides in plan)
    return pl.pallas_call(
        functools.partial(projection_kernel, plan),
        out_shape=[jax.ShapeDtypeStruct((SPAN + TAIL, cols), jnp.float32)] * pieces,
        in_specs=[pl.BlockSpec(memory_space=pltpu.SMEM)] + [vmem] * len(operands),
        out_specs=[vmem] * pieces,
        scratch_shapes=[
            pltpu.VMEM((SPAN, width), jnp.bfloat16),
            pltpu.VMEM((2, width, cols), jnp.bfloat16),
        ],
        compiler_params=pltpu.CompilerParams(vmem_limit_bytes=32 * MIB),
        cost_estimate=pl.CostEstimate(
            flops=pieces * SPAN * width * 2 * cols, bytes_accessed=4 * MIB, transcendentals=0
        ),
    )(counts, *operands)


def finish_kernel(depth, block, ours, theirs, out):
    total = block[0:SPAN, :]
    tail = block[SPAN : SPAN + TAIL, :]
    for message in (ours, theirs):
        total = total + message[0:SPAN, :].astype(jnp.float32)
        tail = tail + message_tail(message)
    fill = jnp.zeros((128 - TAIL, 128), jnp.float32)
    columns = jnp.concatenate(
        [
            jnp.transpose(jnp.concatenate([tail[:, at : at + 128], fill], axis=0))
            for at in (0, 128)
        ],
        axis=0,
    )[:SPAN]
    mean = columns[:, 0:1] / depth
    var = columns[:, 1:2] / depth - mean * mean
    out[...] = ((total - mean * tail[2:3]) * lax.rsqrt(var + epsilon) + tail[3:4]).astype(
        jnp.bfloat16
    )


def finish(block, ours, theirs, depth):
    vmem = pl.BlockSpec(memory_space=pltpu.VMEM)
    return pl.pallas_call(
        functools.partial(finish_kernel, depth),
        out_shape=jax.ShapeDtypeStruct((SPAN, block.shape[1]), jnp.bfloat16),
        in_specs=[vmem] * 3,
        out_specs=vmem,
        compiler_params=pltpu.CompilerParams(vmem_limit_bytes=16 * MIB),
        cost_estimate=pl.CostEstimate(
            flops=4 * SPAN * block.shape[1], bytes_accessed=2 * MIB, transcendentals=SPAN
        ),
    )(block, ours, theirs)


def merge_kernel(counts, rows, rows_far, out):
    low = lax.axis_index("store") < 2
    live = (counts[0] + counts[1]) // 8
    lower = jnp.where(low, rows[...], rows_far[...])
    higher = jnp.where(low, rows_far[...], rows[...])
    edge = BLOCK - SPAN
    place = lax.broadcasted_iota(jnp.int32, (SPAN - edge, rows.shape[1]), 0) + edge
    out[0:edge, :] = lower[:edge]
    out[edge:SPAN, :] = jnp.where(
        place < live, lower[edge:].astype(jnp.float32), higher[: SPAN - edge].astype(jnp.float32)
    ).astype(jnp.bfloat16)
    out[SPAN:BLOCK, :] = higher[SPAN - edge :]


def merge(counts, rows, rows_far):
    vmem = pl.BlockSpec(memory_space=pltpu.VMEM)
    return pl.pallas_call(
        merge_kernel,
        out_shape=jax.ShapeDtypeStruct((BLOCK, rows.shape[1]), jnp.bfloat16),
        in_specs=[pl.BlockSpec(memory_space=pltpu.SMEM)] + [vmem] * 2,
        out_specs=vmem,
        compiler_params=pltpu.CompilerParams(vmem_limit_bytes=16 * MIB),
        cost_estimate=pl.CostEstimate(
            flops=BLOCK * rows.shape[1], bytes_accessed=MIB, transcendentals=0
        ),
    )(counts, rows, rows_far)


def relay_kernel(received, block, out):
    put_message(
        out,
        received[0:SPAN, :].astype(jnp.float32) + block[0:SPAN, :],
        message_tail(received) + block[SPAN : SPAN + TAIL, :],
    )


def relay(received, block):
    vmem = pl.BlockSpec(memory_space=pltpu.VMEM)
    return pl.pallas_call(
        relay_kernel,
        out_shape=jax.ShapeDtypeStruct(received.shape, received.dtype),
        in_specs=[vmem] * 2,
        out_specs=vmem,
        compiler_params=pltpu.CompilerParams(vmem_limit_bytes=16 * MIB),
        cost_estimate=pl.CostEstimate(
            flops=2 * SPAN * block.shape[1], bytes_accessed=2 * MIB, transcendentals=0
        ),
    )(received, block)


def pack_shift(top):
    rows = top.shape[0]
    lane = lax.broadcasted_iota(jnp.int32, (rows, HD), 1)
    left = -jnp.broadcast_to(top, (rows, HD))
    packed = jnp.zeros((rows, HD), jnp.float32)
    for i, piece in enumerate(split(left)):
        packed = jnp.where(lane == i, piece.astype(jnp.float32), packed)
    return packed.astype(jnp.bfloat16)


def own_kernel(q, own_k, own_v, out, shift):
    requests, positions, width = q.shape
    row = lax.broadcasted_iota(jnp.int32, (positions, positions), 0)
    column = lax.broadcasted_iota(jnp.int32, (positions, positions), 1)
    ones = jnp.ones((positions, HD), jnp.bfloat16)
    for head in range(width // HD):
        columns = slice(head * HD, (head + 1) * HD)
        for r in range(requests):
            at = r * positions
            scores = lax.dot_general(
                q[r, :, columns],
                own_k[r, :, columns],
                (((1,), (1,)), ((), ())),
                preferred_element_type=jnp.float32,
            )
            scores = jnp.where(column <= row, scores, -jnp.inf)
            top = jnp.max(scores, axis=1, keepdims=True)
            weights = jnp.exp2((scores - top) * RATE).astype(jnp.bfloat16)
            both = jnp.concatenate([own_v[r, :, columns], ones], axis=1)
            out[head, at : at + positions, :] = jnp.dot(
                weights, both, preferred_element_type=jnp.float32
            )
            shift[head, at : at + positions, :] = pack_shift(top)


def stage_kernel(end, pair_count, *refs):
    refs = list(refs)
    lengths = refs.pop(0) if end else None
    q, state, shift = refs[:3]
    blocks = refs[3 : 3 + 4 * pair_count]
    outs = refs[3 + 4 * pair_count :]
    if end:
        out, done, semaphores = outs

        def copy_out(head):
            columns = pl.ds(head * HD, HD)
            return pltpu.make_async_copy(
                done.at[:, :, columns], out.at[:, :, columns], semaphores.at[head]
            )

    requests, positions, width = q.shape
    rows = requests * positions
    heads = width // HD
    first_core = lax.rem(lax.axis_index("store"), 2) == 0
    ones = jnp.ones((BLOCK * pair_count, HD), jnp.bfloat16)

    def pick(first, columns):
        return jnp.concatenate(
            [
                jnp.where(first_core, blocks[i][:, columns], blocks[i + 1][:, columns])
                for i in range(first, 4 * pair_count, 4)
            ],
            axis=0,
        )

    def shifted_scores(head, columns):
        queries = jnp.concatenate([q[:, :, columns].reshape(rows, HD), shift[head]], axis=1)
        keys = jnp.concatenate([pick(0, columns), ones], axis=1)
        return lax.dot_general(
            queries, keys, (((1,), (1,)), ((), ())), preferred_element_type=jnp.float32
        )

    def weigh(scores, columns):
        weights = jnp.exp2(scores * RATE).astype(jnp.bfloat16)
        values = jnp.concatenate([pick(2, columns), ones], axis=1)
        return jnp.dot(weights, values, preferred_element_type=jnp.float32)

    def emit(head, columns, total, packed):
        if end:
            scale = pl.reciprocal(total[:, HD:], approx=True)
            scale = scale * (2.0 - total[:, HD:] * scale)
            result = total[:, :HD] * scale
            place = lax.broadcasted_iota(jnp.int32, (positions, HD), 0)
            for r in range(requests):
                part = result[r * positions : (r + 1) * positions]
                done[r, :, columns] = jnp.where(place < lengths[r], part, 0.0).astype(jnp.bfloat16)
        else:
            outs[0][head] = total
            outs[1][head] = packed

    largest = jnp.zeros((8, HD), jnp.float32)
    for head in range(heads):
        columns = slice(head * HD, (head + 1) * HD)
        total = state[head] + weigh(shifted_scores(head, columns), columns)
        emit(head, columns, total, shift[head])
        if end:
            copy_out(head).start()
        largest = jnp.maximum(
            largest, jnp.max(total[:, HD:].reshape(rows // 8, 8, HD), axis=0)
        )
    if end:
        for head in range(heads):
            copy_out(head).wait()

    @pl.when(jnp.logical_not(jnp.max(largest) < 1e30))
    def _():
        def one_head(head, carry):
            columns = pl.ds(pl.multiple_of(head * HD, HD), HD)
            scores = shifted_scores(head, columns)
            old = -jnp.sum(shift[head].astype(jnp.float32), axis=1, keepdims=True)
            new = old + jnp.maximum(jnp.max(scores, axis=1, keepdims=True), 0.0)
            moved = new - old
            total = state[head] * jnp.exp2(-moved * RATE) + weigh(scores - moved, columns)
            emit(head, columns, total, pack_shift(new))
            return carry

        lax.fori_loop(0, heads, one_head, 0)
        if end:
            for head in range(heads):
                copy_out(head).start()
            for head in range(heads):
                copy_out(head).wait()


def attend_own(q, k, v):
    requests, positions, width = q.shape
    rows = requests * positions
    heads = width // HD
    vmem = pl.BlockSpec(memory_space=pltpu.VMEM)
    return pl.pallas_call(
        own_kernel,
        out_shape=[
            jax.ShapeDtypeStruct((heads, rows, 2 * HD), jnp.float32),
            jax.ShapeDtypeStruct((heads, rows, HD), jnp.bfloat16),
        ],
        in_specs=[vmem] * 3,
        out_specs=[vmem] * 2,
        compiler_params=pltpu.CompilerParams(vmem_limit_bytes=32 * MIB),
        cost_estimate=pl.CostEstimate(
            flops=4 * rows * positions * width,
            bytes_accessed=6 * MIB,
            transcendentals=rows * positions * heads,
        ),
    )(q, k, v)


def attend(q, state, pairs, lengths=None):
    requests, positions, width = q.shape
    rows = requests * positions
    vmem = pl.BlockSpec(memory_space=pltpu.VMEM)
    operands = [q, *state] + [array for pair in pairs for array in pair]
    specs = [vmem] * len(operands)
    if lengths is not None:
        specs = [pl.BlockSpec(memory_space=pltpu.SMEM)] + specs
        operands = [lengths] + operands
        out_shape = jax.ShapeDtypeStruct(q.shape, jnp.bfloat16)
        out_specs = pl.BlockSpec(memory_space=pl.ANY)
        scratch = [
            pltpu.VMEM(q.shape, jnp.bfloat16),
            pltpu.SemaphoreType.DMA((width // HD,)),
        ]
    else:
        scratch = []
        out_shape = [jax.ShapeDtypeStruct(array.shape, array.dtype) for array in state]
        out_specs = [vmem] * 2
    key_rows = BLOCK * len(pairs)
    return pl.pallas_call(
        functools.partial(stage_kernel, lengths is not None, len(pairs)),
        out_shape=out_shape,
        in_specs=specs,
        out_specs=out_specs,
        scratch_shapes=scratch,
        compiler_params=pltpu.CompilerParams(vmem_limit_bytes=32 * MIB),
        cost_estimate=pl.CostEstimate(
            flops=4 * rows * key_rows * width,
            bytes_accessed=8 * MIB,
            transcendentals=rows * key_rows * width // HD,
        ),
    )(*operands)


def per_device(
    hidden,
    row_counts,
    ln_gain,
    ln_bias,
    key_weight,
    value_weight,
    suffix_q,
    suffix_k,
    suffix_v,
    suffix_lengths,
):
    store = lax.axis_index("store")
    stores = lax.axis_size("store")
    ring = lax.axis_size("req")
    depth = ring * key_weight.shape[0]
    around = [
        (s * ring + z, s * ring + (z + (1 if s % 2 == 0 else ring - 1)) % ring)
        for s in range(stores)
        for z in range(ring)
    ]
    across = [(s, s + 1 - 2 * (s % 2)) for s in range(stores)]
    far = [(s, (s + 2) % 4) for s in range(stores)]

    def step(array):
        return lax.ppermute(array, ("store", "req"), around)

    def swap(array):
        return lax.ppermute(array, "store", across)

    other_hidden = swap(hidden)
    weights = (key_weight, value_weight)
    affine = affine_rows(row_counts, hidden, ln_gain, ln_bias)
    inputs = (row_counts, hidden, other_hidden, ln_gain)
    total, affine_0 = open_chain(4, 0, *inputs, affine, *weights)
    rest, affine_1 = open_chain(3, 1, *inputs, affine, *weights)
    total = step(total)
    rest = step(rest)
    f1, f2, s2, f3, s3, f4 = project_rows(
        ((3, (0,)), (2, (0, 1)), (1, (0, 1)), (0, (0,))),
        *inputs,
        *weights,
        affine_0,
        affine_1,
    )

    total = relay(total, f1)
    rest = relay(rest, s2)
    total = relay(step(total), f2)
    rest = relay(step(rest), s3)
    total = step(relay(step(total), f3))
    rows = finish(f4, total, swap(step(rest)), depth)

    mine = merge(row_counts, rows, lax.ppermute(rows, "store", far))

    other = swap(mine)
    g1 = step(mine)
    h1 = step(other)
    state = attend_own(suffix_q, suffix_k, suffix_v)
    g1, state = lax.optimization_barrier((g1, state))
    xg1 = swap(g1)
    g2 = step(g1)
    xh1 = swap(h1)
    h2 = step(h1)
    xg2 = swap(g2)
    xh2 = swap(h2)
    g3 = step(g2)

    def upper(g, xg, h, xh):
        return (g, xg, h, xh)

    def lower(g, xg, h, xh):
        return (xh, h, xg, g)

    h2, state = lax.optimization_barrier((h2, state))
    h3 = step(h2)
    near = (g1, xg1, h1, xh1)
    state = attend(
        suffix_q, state, [(mine, other, other, mine), upper(*near), lower(*near)]
    )
    g3, state = lax.optimization_barrier((g3, state))
    xg3 = swap(g3)
    g4 = step(g3)
    near = (g2, xg2, h2, xh2)
    state = attend(suffix_q, state, [upper(*near), lower(*near)])
    xh3 = swap(h3)
    g4, state = lax.optimization_barrier((g4, state))
    xg4 = swap(g4)
    near = (g3, xg3, h3, xh3)
    state = attend(suffix_q, state, [upper(*near), lower(*near)])
    return attend(suffix_q, state, [(g4, xg4, xg4, g4)], lengths=suffix_lengths)


def solution(mesh):
    in_specs = (
        P("store", "req"),
        P(),
        P("req"),
        P("req"),
        P("req", "tp"),
        P("req", "tp"),
        P(("store", "req"), None, "tp"),
        P(("store", "req"), None, "tp"),
        P(("store", "req"), None, "tp"),
        P(("store", "req")),
    )
    out_specs = P(("store", "req"), None, "tp")
    return jax.shard_map(
        per_device, mesh=mesh, in_specs=in_specs, out_specs=out_specs, check_vma=False
    )
```
